32 devices in a mesh: row: 4 (over z), col: 4 (over y, x), layer: 2 (over core).
Axes of the slice: x: 2, y: 2, z: 4, core: 2. Of those that a mesh axis runs over, the one named last changes fastest.
Arguments:
- left_blocks: bfloat16 [1024, 2, 512], P('row', 'layer', 'col'), may hold values from 3.886223e-05 to 0.00390625
- batch_blocks: bfloat16 [2, 512, 2048], P('layer', 'row', 'col'), may hold values from 0.019897461 to 2
- left_mask: int32 [8, 2, 4], P('row', 'layer', 'col'), may hold values 0 or 1
- batch_mask: int32 [2, 4, 16], P('layer', 'row', 'col'), may hold values 0 or 1
- prune_mask: int32 [8, 16], P('row', ('col', 'layer')), may hold values 0 or 1
Outputs:
- normalized: float32 [1024, 2048], P('row', ('col', 'layer'))
The draws below stay inside these ranges and needn't reach their ends.
All inputs are finite; a program needn't handle non-finite values. No bound on the sum of `left_mask` or of `batch_mask` or of `prune_mask` on one device may be relied on, other than what follows from the above.
Results may differ from the reference program's by a relative error of at most 0.0003.
Values may be sent and summed in bfloat16 or wider, within the bound.
No kernel may reach another device: no remote copies, remote signals or barrier semaphores. Data moves between devices by JAX's collectives and lax.ppermute only.
A program may use at most 64 MiB of HBM per device.

```python
import math
import jax
import jax.numpy as jnp

M = 1024
KH = 512
NB = 2048
MT = 8
KT = 4
NBT = 16


def with_ends(values, own_key, low, high):
    spot = [jax.random.randint(jax.random.fold_in(own_key, axis), (), 0, length) for axis, length in enumerate(values.shape)]
    longest = values.shape.index(max(values.shape))
    next_to = spot[:longest] + [(spot[longest] + 1) % values.shape[longest]] + spot[longest + 1:]
    return values.at[tuple(spot)].set(low).at[tuple(next_to)].set(high)


def level_of(rng, dims, split, smallest, high):
    loudness, own = 1.0, jax.random.fold_in(rng, 6)
    for axis_at, shards_of in split:
        heights = jnp.exp(jax.random.uniform(jax.random.fold_in(own, axis_at), (shards_of,), jnp.float32, smallest / len(split), high / len(split)))
        loudness = loudness * jnp.repeat(heights, dims[axis_at] // shards_of).reshape([-1 if axis == axis_at else 1 for axis in range(len(dims))])
    return loudness


def setup_inputs(seed: int = 0) -> dict:
    arg_keys = jax.random.split(jax.random.key(seed), 6)
    left_blocks = jnp.clip(jnp.exp(math.log(0.00390625) - 4.61031033 * jax.random.uniform(arg_keys[0], (M, 2, KH), jnp.float32) ** level_of(arg_keys[0], (M, 2, KH), ((0, 4), (1, 2), (2, 4)), -0.2, 0.2)), 3.886222839355469e-05, 0.00390625).astype(jnp.bfloat16)
    batch_blocks = jnp.clip(jnp.exp(math.log(2.0) - 4.61031033 * jax.random.uniform(arg_keys[1], (2, KH, NB), jnp.float32) ** level_of(arg_keys[1], (2, KH, NB), ((0, 2), (1, 4), (2, 4)), -0.2, 0.2)), 0.019897461, 2.0).astype(jnp.bfloat16)
    left_mask = with_ends((jax.random.randint(arg_keys[2], (MT, 2, KT), 0, 4) < 3).astype(jnp.int32), jax.random.fold_in(arg_keys[2], 1), 0, 1)
    batch_mask = with_ends((jax.random.randint(arg_keys[3], (2, KT, NBT), 0, 4) < 3).astype(jnp.int32), jax.random.fold_in(arg_keys[3], 1), 0, 1)
    prune_mask = with_ends((jax.random.randint(arg_keys[4], (MT, NBT), 0, 3) < 2).astype(jnp.int32), jax.random.fold_in(arg_keys[4], 1), 0, 1)
    return {"left_blocks": left_blocks, "batch_blocks": batch_blocks, "left_mask": left_mask, "batch_mask": batch_mask, "prune_mask": prune_mask}


def widen_left(mask, tile_size):
    first, middle, last = mask.shape
    spread = jnp.broadcast_to(mask.astype(jnp.bfloat16)[:, None, :, :, None], (first, tile_size, middle, last, tile_size))
    return spread.reshape(first * tile_size, middle, last * tile_size)


def widen_right(mask, tile_size):
    first, middle, last = mask.shape
    spread = jnp.broadcast_to(mask.astype(jnp.bfloat16)[:, :, None, :, None], (first, middle, tile_size, last, tile_size))
    return spread.reshape(first, middle * tile_size, last * tile_size)


def widen_pair(mask, tile_size):
    first, last = mask.shape
    spread = jnp.broadcast_to(mask.astype(jnp.float32)[:, None, :, None], (first, tile_size, last, tile_size))
    return spread.reshape(first * tile_size, last * tile_size)


def reference(left_blocks, batch_blocks, left_mask, batch_mask, prune_mask):
    tile_size = left_blocks.shape[0] // left_mask.shape[0]
    left = (left_blocks * widen_left(left_mask, tile_size)).astype(jnp.bfloat16)
    right = (batch_blocks * widen_right(batch_mask, tile_size)).astype(jnp.bfloat16)
    product = jnp.dot(left[:, 0, :], right[0], preferred_element_type=jnp.float32)
    product = product + jnp.dot(left[:, 1, :], right[1], preferred_element_type=jnp.float32)
    inflated = product * product * widen_pair(prune_mask, tile_size)
    col_sums = jnp.sum(inflated, axis=0)
    return inflated * (M / (col_sums + 1e-6))
```

```python
import functools

import jax
import jax.numpy as jnp
from jax import lax
from jax.experimental import pallas as pl
from jax.experimental.pallas import tpu as pltpu
from jax.sharding import PartitionSpec as P

epsilon = 1e-06
SMEM = pl.BlockSpec(memory_space=pltpu.SMEM)
VMEM = pl.BlockSpec(memory_space=pltpu.VMEM)


def mask_kernel(mask, block, out):
    tall, wide = mask.shape
    high, broad = block.shape[0] // tall, block.shape[1] // wide
    for i in range(tall):
        for j in range(wide):
            at = (slice(i * high, (i + 1) * high), slice(j * broad, (j + 1) * broad))
            values = block[at]
            out[at] = jnp.where(mask[i, j] != 0, values, jnp.zeros_like(values))


def masked(mask, block):
    return pl.pallas_call(
        mask_kernel,
        out_shape=jax.ShapeDtypeStruct(block.shape, block.dtype),
        in_specs=[SMEM, VMEM],
        out_specs=VMEM,
        compiler_params=pltpu.CompilerParams(vmem_limit_bytes=4 << 20),
        name="mask_tiles",
    )(mask, block)


def swapped(value, axis, step):
    count = lax.axis_size(axis)
    return lax.ppermute(value, axis, [(i, i ^ step) for i in range(count)])


def product_kernel(place, *refs):
    count = (len(refs) - 3) // 2
    lefts, rights = refs[:count], refs[count : 2 * count]
    keep, give, held = refs[2 * count :]
    for s in range(count):
        held[s] = lefts[s][...]
    half = keep.shape[1]
    mine = pl.multiple_of(place[1] * half, half)
    other = pl.multiple_of((1 - place[1]) * half, half)
    for out, at in ((give, other), (keep, mine)):
        total = jnp.zeros(out.shape, jnp.float32)
        for t in range(count):
            total += jnp.dot(
                held[place[0] ^ t],
                rights[t][:, pl.ds(at, half)],
                preferred_element_type=jnp.float32,
            )
        out[...] = total


def inflate_kernel(mask, keep, got, inflated, sums):
    tall, wide = mask.shape
    high, broad = keep.shape[0] // tall, keep.shape[1] // wide
    for j in range(wide):
        total = jnp.zeros((1, broad), jnp.float32)
        for i in range(tall):
            at = (slice(i * high, (i + 1) * high), slice(j * broad, (j + 1) * broad))
            product = keep[at] + got[at]
            value = jnp.where(mask[i, j] != 0, product * product, 0.0)
            inflated[at] = value
            total += jnp.sum(value, axis=0, keepdims=True)
        sums[:, j * broad : (j + 1) * broad] = total


def on_device(left_blocks, batch_blocks, left_mask, batch_mask, prune_mask):
    f32 = jnp.float32
    rows, columns = left_blocks.shape[0], batch_blocks.shape[2]
    half = columns // 2
    left = masked(left_mask[:, 0, :], left_blocks[:, 0, :])
    right = masked(batch_mask[0], batch_blocks[0])
    count = lax.axis_size("row")
    rights = [right] + [swapped(right, "row", s) for s in range(1, count)]
    lefts = [left] + [swapped(left, "col", s) for s in range(1, count)]
    place = jnp.stack(
        [lax.axis_index("row") ^ lax.axis_index("col"), lax.axis_index("layer")]
    ).astype(jnp.int32)
    piece = jax.ShapeDtypeStruct((rows, half), f32)
    keep, give = pl.pallas_call(
        product_kernel,
        out_shape=[piece, piece],
        in_specs=[SMEM] + [VMEM] * (2 * count),
        out_specs=[VMEM, VMEM],
        scratch_shapes=[pltpu.VMEM((count,) + left.shape, left.dtype)],
        compiler_params=pltpu.CompilerParams(vmem_limit_bytes=4 << 20),
        name="product",
    )(place, *lefts, *rights)
    got = swapped(give, "layer", 1)
    inflated, sums = pl.pallas_call(
        inflate_kernel,
        out_shape=[piece, jax.ShapeDtypeStruct((1, half), f32)],
        in_specs=[SMEM, VMEM, VMEM],
        out_specs=[VMEM, VMEM],
        compiler_params=pltpu.CompilerParams(vmem_limit_bytes=4 << 20),
        name="inflate",
    )(prune_mask, keep, got)
    for s in (1, 2):
        sums = sums + swapped(sums, "row", s)
    total_rows = rows * count
    return inflated * (total_rows / (sums + epsilon))


def widen(mask, tile_size, dtype):
    first, last = mask.shape
    spread = jnp.broadcast_to(
        mask.astype(dtype)[:, None, :, None], (first, tile_size, last, tile_size)
    )
    return spread.reshape(first * tile_size, last * tile_size)


def on_any_device(left_blocks, batch_blocks, left_mask, batch_mask, prune_mask):
    tile_size = left_blocks.shape[0] // left_mask.shape[0]
    left = left_blocks[:, 0, :] * widen(left_mask[:, 0, :], tile_size, jnp.bfloat16)
    right = batch_blocks[0] * widen(batch_mask[0], tile_size, jnp.bfloat16)
    product = jnp.dot(
        lax.all_gather(left, "col", axis=1, tiled=True),
        lax.all_gather(right, "row", axis=0, tiled=True),
        preferred_element_type=jnp.float32,
    )
    own_share = lax.psum_scatter(product, "layer", scatter_dimension=1, tiled=True)
    inflated = own_share * own_share * widen(prune_mask, tile_size, jnp.float32)
    col_sums = lax.psum(jnp.sum(inflated, axis=0), "row")
    total_rows = left.shape[0] * lax.axis_size("row")
    return inflated * (total_rows / (col_sums + epsilon))


def solution(mesh):
    placed = (
        P("row", "layer", "col"),
        P("layer", "row", "col"),
        P("row", "layer", "col"),
        P("layer", "row", "col"),
        P("row", ("col", "layer")),
    )
    small = mesh.shape["row"] == 4 and mesh.shape["col"] == 4 and mesh.shape["layer"] == 2
    return jax.shard_map(
        on_device if small else on_any_device,
        mesh=mesh,
        in_specs=placed,
        out_specs=P("row", ("col", "layer")),
        check_vma=False,
    )
```

```python
import functools

import jax
import jax.numpy as jnp
from jax import lax
from jax.experimental import pallas as pl
from jax.experimental.pallas import tpu as pltpu
from jax.sharding import PartitionSpec as P

epsilon = 1e-06
VMEM = pl.BlockSpec(memory_space=pltpu.VMEM)
room = pltpu.CompilerParams(vmem_limit_bytes=4 << 20)


def entry(mask, i, j):
    return mask[i : i + 1, j : j + 1] != 0


def keep_tiles(mask, turned, block, out):
    tall, wide = mask.shape[::-1] if turned else mask.shape
    high, broad = block.shape[0] // tall, block.shape[1] // wide
    for i in range(tall):
        for j in range(wide):
            at = (slice(i * high, (i + 1) * high), slice(j * broad, (j + 1) * broad))
            values = block[at]
            one = entry(mask, j, i) if turned else entry(mask, i, j)
            kept = jnp.broadcast_to(one, values.shape)
            out[at] = jnp.where(kept, values, jnp.zeros_like(values))


def tiles_kernel(*refs):
    operands, (right, left), held, arrived = refs[:4], refs[4:6], refs[6:10], refs[10]
    copies = [
        pltpu.make_async_copy(operands[n], held[n], arrived.at[n]) for n in range(4)
    ]
    for copy in copies:
        copy.start()
    copies[0].wait()
    copies[1].wait()
    keep_tiles(held[0], False, held[1], right)
    copies[2].wait()
    copies[3].wait()
    keep_tiles(held[2], True, held[3], left)


def tiles(*operands):
    held = [pltpu.VMEM(value.shape, value.dtype) for value in operands]
    return pl.pallas_call(
        tiles_kernel,
        out_shape=[
            jax.ShapeDtypeStruct(operands[n].shape, operands[n].dtype) for n in (1, 3)
        ],
        in_specs=[pl.BlockSpec(memory_space=pltpu.HBM)] * 4,
        out_specs=[VMEM, VMEM],
        scratch_shapes=held + [pltpu.SemaphoreType.DMA((4,))],
        compiler_params=room,
        name="tiles",
    )(*(pltpu.with_memory_space_constraint(value, pltpu.HBM) for value in operands))


def call(kernel, name, shapes, *operands, scratch=()):
    return pl.pallas_call(
        kernel,
        out_shape=shapes,
        in_specs=[VMEM] * len(operands),
        out_specs=jax.tree.map(lambda _: VMEM, shapes),
        scratch_shapes=scratch,
        compiler_params=room,
        name=name,
    )(*operands)


def swapped(value, axis, step):
    count = lax.axis_size(axis)
    return lax.ppermute(value, axis, [(i, i ^ step) for i in range(count)])


def product_kernel(*refs):
    count = (len(refs) - 3) // 2
    lefts, rights = refs[:count], refs[count : 2 * count]
    keep, give, held = refs[2 * count :]
    for s in range(count):
        held[s] = lefts[s][...]
    apart = lax.axis_index("row") ^ lax.axis_index("col")
    layer = lax.axis_index("layer")
    half = keep.shape[1]
    mine = pl.multiple_of(layer * half, half)
    other = pl.multiple_of((1 - layer) * half, half)
    for out, at in ((give, other), (keep, mine)):
        total = jnp.zeros(out.shape, jnp.float32)
        for t in range(count):
            total += jnp.dot(
                held[apart ^ t],
                rights[t][:, pl.ds(at, half)],
                preferred_element_type=jnp.float32,
            )
        out[...] = total


def inflate_kernel(mask, mine, got, out, sums):
    tall, wide = mask.shape
    high, broad = mine.shape[0] // tall, mine.shape[1] // wide
    for j in range(wide):
        total = jnp.zeros((1, broad), jnp.float32)
        columns = slice(j * broad, (j + 1) * broad)
        for i in range(tall):
            at = (slice(i * high, (i + 1) * high), columns)
            product = mine[at] + got[at]
            kept = jnp.broadcast_to(entry(mask, i, j), product.shape)
            value = jnp.where(kept, product * product, 0.0)
            out[at] = value
            total += jnp.sum(value, axis=0, keepdims=True)
        sums[:, columns] = total


def on_device(left_blocks, batch_blocks, left_mask, batch_mask, prune_mask):
    f32 = jnp.float32
    rows, columns = left_blocks.shape[0], batch_blocks.shape[2]
    half = columns // 2
    right, left = tiles(
        batch_mask[0],
        batch_blocks[0],
        jnp.transpose(left_mask, (1, 2, 0))[0],
        left_blocks[:, 0, :],
    )
    count = lax.axis_size("row")
    rights = [right] + [swapped(right, "row", s) for s in range(1, count)]
    lefts = [left, swapped(left, "col", 1), swapped(left, "col", 2)]
    lefts.append(swapped(lefts[1], "col", 2))
    piece = jax.ShapeDtypeStruct((rows, half), f32)
    keep, give = call(
        product_kernel,
        "product",
        [piece, piece],
        *lefts,
        *rights,
        scratch=[pltpu.VMEM((count,) + left.shape, left.dtype)],
    )
    got = swapped(give, "layer", 1)
    inflated, sums = call(
        inflate_kernel,
        "inflate",
        [piece, jax.ShapeDtypeStruct((1, half), f32)],
        prune_mask,
        keep,
        got,
    )
    for s in (1, 2):
        sums = sums + swapped(sums, "row", s)
    total_rows = rows * count
    return inflated * (total_rows / (sums + epsilon))


def widen(mask, tile_size, dtype):
    first, last = mask.shape
    spread = jnp.broadcast_to(
        mask.astype(dtype)[:, None, :, None], (first, tile_size, last, tile_size)
    )
    return spread.reshape(first * tile_size, last * tile_size)


def on_any_device(left_blocks, batch_blocks, left_mask, batch_mask, prune_mask):
    tile_size = left_blocks.shape[0] // left_mask.shape[0]
    left = left_blocks[:, 0, :] * widen(left_mask[:, 0, :], tile_size, jnp.bfloat16)
    right = batch_blocks[0] * widen(batch_mask[0], tile_size, jnp.bfloat16)
    product = jnp.dot(
        lax.all_gather(left, "col", axis=1, tiled=True),
        lax.all_gather(right, "row", axis=0, tiled=True),
        preferred_element_type=jnp.float32,
    )
    own_share = lax.psum_scatter(product, "layer", scatter_dimension=1, tiled=True)
    inflated = own_share * own_share * widen(prune_mask, tile_size, jnp.float32)
    col_sums = lax.psum(jnp.sum(inflated, axis=0), "row")
    total_rows = left.shape[0] * lax.axis_size("row")
    return inflated * (total_rows / (col_sums + epsilon))


def solution(mesh):
    placed = (
        P("row", "layer", "col"),
        P("layer", "row", "col"),
        P("row", "layer", "col"),
        P("layer", "row", "col"),
        P("row", ("col", "layer")),
    )
    small = mesh.shape["row"] == 4 and mesh.shape["col"] == 4 and mesh.shape["layer"] == 2
    return jax.shard_map(
        on_device if small else on_any_device,
        mesh=mesh,
        in_specs=placed,
        out_specs=P("row", ("col", "layer")),
        check_vma=False,
    )
```

```python
import functools

import jax
import jax.numpy as jnp
from jax import lax
from jax.experimental import pallas as pl
from jax.experimental.pallas import tpu as pltpu
from jax.sharding import PartitionSpec as P

epsilon = 1e-06
VMEM = pl.BlockSpec(memory_space=pltpu.VMEM)
room = pltpu.CompilerParams(vmem_limit_bytes=4 << 20)


def entry(mask, i, j):
    return mask[i : i + 1, j : j + 1] != 0


def keep_tiles(mask, turned, block, out):
    tall, wide = mask.shape[::-1] if turned else mask.shape
    high, broad = block.shape[0] // tall, block.shape[1] // wide
    for i in range(tall):
        for j in range(wide):
            at = (slice(i * high, (i + 1) * high), slice(j * broad, (j + 1) * broad))
            values = block[at]
            one = entry(mask, j, i) if turned else entry(mask, i, j)
            kept = jnp.broadcast_to(one, values.shape)
            out[at] = jnp.where(kept, values, jnp.zeros_like(values))


def tiles_kernel(*refs):
    operands, (right, left), held, arrived = refs[:4], refs[4:6], refs[6:10], refs[10]
    copies = [
        pltpu.make_async_copy(operands[n], held[n], arrived.at[n]) for n in range(4)
    ]
    for copy in copies:
        copy.start()
    copies[0].wait()
    copies[1].wait()
    keep_tiles(held[0], False, held[1], right)
    copies[2].wait()
    copies[3].wait()
    keep_tiles(held[2], True, held[3], left)


def tiles(*operands):
    held = [pltpu.VMEM(value.shape, value.dtype) for value in operands]
    return pl.pallas_call(
        tiles_kernel,
        out_shape=[
            jax.ShapeDtypeStruct(operands[n].shape, operands[n].dtype) for n in (1, 3)
        ],
        in_specs=[pl.BlockSpec(memory_space=pltpu.HBM)] * 4,
        out_specs=[VMEM, VMEM],
        scratch_shapes=held + [pltpu.SemaphoreType.DMA((4,))],
        compiler_params=room,
        name="tiles",
    )(*(pltpu.with_memory_space_constraint(value, pltpu.HBM) for value in operands))


def call(kernel, name, shapes, *operands, scratch=()):
    return pl.pallas_call(
        kernel,
        out_shape=shapes,
        in_specs=[VMEM] * len(operands),
        out_specs=jax.tree.map(lambda _: VMEM, shapes),
        scratch_shapes=scratch,
        compiler_params=room,
        name=name,
    )(*operands)


def swapped(value, axis, step):
    count = lax.axis_size(axis)
    return lax.ppermute(value, axis, [(i, i ^ step) for i in range(count)])


def product_kernel(*refs):
    lefts, rights, (keep, give, held) = refs[:4], refs[4:9], refs[9:]
    for s in range(4):
        held[s] = lefts[s][...]
    row, col = lax.axis_index("row"), lax.axis_index("col")
    layer = lax.axis_index("layer")
    half = keep.shape[1]
    mine = pl.multiple_of(layer * half, half)
    other = pl.multiple_of((1 - layer) * half, half)
    first = lax.rem(2 * row + 1, 5)
    inner = jnp.logical_or(row == 1, row == 2)
    blocks = (row, first, first ^ 3, row ^ 3)
    for out, at in ((give, other), (keep, mine)):
        total = jnp.zeros(out.shape, jnp.float32)
        for t in range(4):
            block = rights[t][:, pl.ds(at, half)]
            if t == 3:
                block = jnp.where(inner, block, rights[4][:, pl.ds(at, half)])
            total += jnp.dot(
                held[blocks[t] ^ col], block, preferred_element_type=jnp.float32
            )
        out[...] = total


def inflate_kernel(mask, mine, got, out, sums):
    tall, wide = mask.shape
    high, broad = mine.shape[0] // tall, mine.shape[1] // wide
    for j in range(wide):
        total = jnp.zeros((1, broad), jnp.float32)
        columns = slice(j * broad, (j + 1) * broad)
        for i in range(tall):
            at = (slice(i * high, (i + 1) * high), columns)
            product = mine[at] + got[at]
            kept = jnp.broadcast_to(entry(mask, i, j), product.shape)
            value = jnp.where(kept, product * product, 0.0)
            out[at] = value
            total += jnp.sum(value, axis=0, keepdims=True)
        sums[:, columns] = total


def on_device(left_blocks, batch_blocks, left_mask, batch_mask, prune_mask):
    f32 = jnp.float32
    rows, columns = left_blocks.shape[0], batch_blocks.shape[2]
    half = columns // 2
    right, left = tiles(
        batch_mask[0],
        batch_blocks[0],
        jnp.transpose(left_mask, (1, 2, 0))[0],
        left_blocks[:, 0, :],
    )
    count = lax.axis_size("row")
    first = lax.ppermute(right, "row", [(0, 2), (3, 1), (1, 0), (2, 3)])
    second = lax.ppermute(right, "row", [(0, 1), (3, 2), (1, 3), (2, 0)])
    pairs = [(2, 4), (3, 5), (4, 2), (5, 3), (0, 1), (1, 0), (6, 7), (7, 6)]
    inner = lax.ppermute(right, ("row", "layer"), pairs)
    outer = lax.ppermute(first, "row", [(0, 1), (1, 0), (2, 3), (3, 2)])
    rights = [right, first, second, inner, outer]
    lefts = [left, swapped(left, "col", 1), swapped(left, "col", 2)]
    lefts.append(swapped(lefts[1], "col", 2))
    piece = jax.ShapeDtypeStruct((rows, half), f32)
    keep, give = call(
        product_kernel,
        "product",
        [piece, piece],
        *lefts,
        *rights,
        scratch=[pltpu.VMEM((count,) + left.shape, left.dtype)],
    )
    got = swapped(give, "layer", 1)
    inflated, sums = call(
        inflate_kernel,
        "inflate",
        [piece, jax.ShapeDtypeStruct((1, half), f32)],
        prune_mask,
        keep,
        got,
    )
    for s in (1, 2):
        sums = sums + swapped(sums, "row", s)
    total_rows = rows * count
    return inflated * (total_rows / (sums + epsilon))


def widen(mask, tile_size, dtype):
    first, last = mask.shape
    spread = jnp.broadcast_to(
        mask.astype(dtype)[:, None, :, None], (first, tile_size, last, tile_size)
    )
    return spread.reshape(first * tile_size, last * tile_size)


def on_any_device(left_blocks, batch_blocks, left_mask, batch_mask, prune_mask):
    tile_size = left_blocks.shape[0] // left_mask.shape[0]
    left = left_blocks[:, 0, :] * widen(left_mask[:, 0, :], tile_size, jnp.bfloat16)
    right = batch_blocks[0] * widen(batch_mask[0], tile_size, jnp.bfloat16)
    product = jnp.dot(
        lax.all_gather(left, "col", axis=1, tiled=True),
        lax.all_gather(right, "row", axis=0, tiled=True),
        preferred_element_type=jnp.float32,
    )
    own_share = lax.psum_scatter(product, "layer", scatter_dimension=1, tiled=True)
    inflated = own_share * own_share * widen(prune_mask, tile_size, jnp.float32)
    col_sums = lax.psum(jnp.sum(inflated, axis=0), "row")
    total_rows = left.shape[0] * lax.axis_size("row")
    return inflated * (total_rows / (col_sums + epsilon))


def solution(mesh):
    placed = (
        P("row", "layer", "col"),
        P("layer", "row", "col"),
        P("row", "layer", "col"),
        P("layer", "row", "col"),
        P("row", ("col", "layer")),
    )
    small = mesh.shape["row"] == 4 and mesh.shape["col"] == 4 and mesh.shape["layer"] == 2
    return jax.shard_map(
        on_device if small else on_any_device,
        mesh=mesh,
        in_specs=placed,
        out_specs=P("row", ("col", "layer")),
        check_vma=False,
    )
```

```python
import functools

import jax
import jax.numpy as jnp
from jax import lax
from jax.experimental import pallas as pl
from jax.experimental.pallas import tpu as pltpu
from jax.sharding import PartitionSpec as P

epsilon = 1e-06
VMEM = pl.BlockSpec(memory_space=pltpu.VMEM)
room = pltpu.CompilerParams(vmem_limit_bytes=4 << 20)


def entry(mask, i, j):
    return mask[i : i + 1, j : j + 1] != 0


def keep_tiles(mask, turned, block, out):
    tall, wide = mask.shape[::-1] if turned else mask.shape
    high, broad = block.shape[0] // tall, block.shape[1] // wide
    for i in range(tall):
        for j in range(wide):
            at = (slice(i * high, (i + 1) * high), slice(j * broad, (j + 1) * broad))
            values = block[at]
            one = entry(mask, j, i) if turned else entry(mask, i, j)
            kept = jnp.broadcast_to(one, values.shape)
            out[at] = jnp.where(kept, values, jnp.zeros_like(values))


def tiles_kernel(*refs):
    operands, (right, left), held, arrived = refs[:4], refs[4:6], refs[6:10], refs[10]
    copies = [
        pltpu.make_async_copy(operands[n], held[n], arrived.at[n]) for n in range(4)
    ]
    for copy in copies:
        copy.start()
    copies[0].wait()
    copies[1].wait()
    keep_tiles(held[0], False, held[1], right)
    copies[2].wait()
    copies[3].wait()
    keep_tiles(held[2], True, held[3], left)


def tiles(*operands):
    held = [pltpu.VMEM(value.shape, value.dtype) for value in operands]
    return pl.pallas_call(
        tiles_kernel,
        out_shape=[
            jax.ShapeDtypeStruct(operands[n].shape, operands[n].dtype) for n in (1, 3)
        ],
        in_specs=[pl.BlockSpec(memory_space=pltpu.HBM)] * 4,
        out_specs=[VMEM, VMEM],
        scratch_shapes=held + [pltpu.SemaphoreType.DMA((4,))],
        compiler_params=room,
        name="tiles",
    )(*(pltpu.with_memory_space_constraint(value, pltpu.HBM) for value in operands))


def call(kernel, name, shapes, *operands, scratch=()):
    return pl.pallas_call(
        kernel,
        out_shape=shapes,
        in_specs=[VMEM] * len(operands),
        out_specs=jax.tree.map(lambda _: VMEM, shapes),
        scratch_shapes=scratch,
        compiler_params=room,
        name=name,
    )(*operands)


def swapped(value, axis, step):
    count = lax.axis_size(axis)
    return lax.ppermute(value, axis, [(i, i ^ step) for i in range(count)])


def pair_kernel(here, beside, out):
    out[0] = here[...]
    out[1] = beside[...]


def product_kernel(near, far, *refs):
    rights, (mask, partial, held) = refs[:5], refs[5:]
    held[0:2] = near[...]
    held[2:4] = far[...]
    row, col = lax.axis_index("row"), lax.axis_index("col")
    first = lax.rem(2 * row + 1, 5)
    inner = jnp.logical_or(row == 1, row == 2)
    blocks = (row, first, first ^ 3, row ^ 3)
    rows, columns = held.shape[1], partial.shape[1]
    total = jnp.zeros((rows, columns), jnp.float32)
    for t in range(4):
        block = rights[t][...]
        if t == 3:
            block = jnp.where(inner, block, rights[4][...])
        total += jnp.dot(
            held[blocks[t] ^ col], block, preferred_element_type=jnp.float32
        )
    partial[0:rows, :] = total
    tall, wide = mask.shape
    broad = columns // 2 // wide
    for i in range(tall):
        for j in range(2 * wide):
            kept = entry(mask, i, j % wide).astype(jnp.float32)
            at = (slice(rows + i, rows + i + 1), slice(j * broad, (j + 1) * broad))
            partial[at] = jnp.broadcast_to(kept, (1, broad))


def inflate_kernel(tall, wide, mine, got, out, sums):
    rows, half = out.shape
    high, broad = rows // tall, half // wide
    layer = lax.axis_index("layer")
    for side in range(2):
        for j in range(wide):
            columns = slice(side * half + j * broad, side * half + (j + 1) * broad)
            total = jnp.zeros((1, broad), jnp.float32)
            for i in range(tall):
                at = (slice(i * high, (i + 1) * high), columns)
                product = mine[at] + got[at]
                entries = (slice(rows + i, rows + i + 1), columns)
                kept = jnp.where(layer == side, mine[entries], got[entries]) != 0.0
                kept = jnp.broadcast_to(kept, product.shape)
                value = jnp.where(kept, product * product, 0.0)
                total += jnp.sum(value, axis=0, keepdims=True)

                @pl.when(layer == side)
                def _():
                    out[at[0], j * broad : (j + 1) * broad] = value

            sums[:, columns] = total


def on_device(left_blocks, batch_blocks, left_mask, batch_mask, prune_mask):
    f32 = jnp.float32
    rows, columns = left_blocks.shape[0], batch_blocks.shape[2]
    half = columns // 2
    right, left = tiles(
        batch_mask[0],
        batch_blocks[0],
        jnp.transpose(left_mask, (1, 2, 0))[0],
        left_blocks[:, 0, :],
    )
    count = lax.axis_size("row")
    first = lax.ppermute(right, "row", [(0, 2), (3, 1), (1, 0), (2, 3)])
    second = lax.ppermute(right, "row", [(0, 1), (3, 2), (1, 3), (2, 0)])
    pairs = [(2, 4), (3, 5), (4, 2), (5, 3), (0, 1), (1, 0), (6, 7), (7, 6)]
    inner = lax.ppermute(right, ("row", "layer"), pairs)
    outer = lax.ppermute(first, "row", [(0, 1), (1, 0), (2, 3), (3, 2)])
    rights = [right, first, second, inner, outer]
    beside = swapped(left, "col", 1)
    pair = call(
        pair_kernel, "pair", jax.ShapeDtypeStruct((2,) + left.shape, left.dtype), left, beside
    )
    lefts = [pair, swapped(pair, "col", 2)]
    piece = jax.ShapeDtypeStruct((rows, half), f32)
    tall, wide = prune_mask.shape
    partial = call(
        product_kernel,
        "product",
        jax.ShapeDtypeStruct((rows + (tall + 7) // 8 * 8, columns), f32),
        *lefts,
        *rights,
        prune_mask,
        scratch=[pltpu.VMEM((4,) + left.shape, left.dtype)],
    )
    got = swapped(partial, "layer", 1)
    inflated, sums = call(
        functools.partial(inflate_kernel, tall, wide),
        "inflate",
        [piece, jax.ShapeDtypeStruct((1, columns), f32)],
        partial,
        got,
    )
    steps = [(2 * z + 1, 2 * (z ^ 1)) for z in range(4)] + [(2 * z, 2 * z + 1) for z in range(4)]
    sums = sums + lax.ppermute(sums, ("row", "layer"), steps)
    steps = [(2 * z, 2 * (z ^ 2) + 1) for z in range(4)] + [(2 * z + 1, 2 * z) for z in range(4)]
    far = lax.ppermute(sums, ("row", "layer"), steps)
    total = far + swapped(sums, "layer", 1)
    total_low = swapped(total, "layer", 1)
    low = lax.axis_index("layer") == 0
    sums = jnp.where(low, total_low[:, :half], total[:, half:])
    total_rows = rows * count
    return inflated * (total_rows / (sums + epsilon))


def widen(mask, tile_size, dtype):
    first, last = mask.shape
    spread = jnp.broadcast_to(
        mask.astype(dtype)[:, None, :, None], (first, tile_size, last, tile_size)
    )
    return spread.reshape(first * tile_size, last * tile_size)


def on_any_device(left_blocks, batch_blocks, left_mask, batch_mask, prune_mask):
    tile_size = left_blocks.shape[0] // left_mask.shape[0]
    left = left_blocks[:, 0, :] * widen(left_mask[:, 0, :], tile_size, jnp.bfloat16)
    right = batch_blocks[0] * widen(batch_mask[0], tile_size, jnp.bfloat16)
    product = jnp.dot(
        lax.all_gather(left, "col", axis=1, tiled=True),
        lax.all_gather(right, "row", axis=0, tiled=True),
        preferred_element_type=jnp.float32,
    )
    own_share = lax.psum_scatter(product, "layer", scatter_dimension=1, tiled=True)
    inflated = own_share * own_share * widen(prune_mask, tile_size, jnp.float32)
    col_sums = lax.psum(jnp.sum(inflated, axis=0), "row")
    total_rows = left.shape[0] * lax.axis_size("row")
    return inflated * (total_rows / (col_sums + epsilon))


def solution(mesh):
    placed = (
        P("row", "layer", "col"),
        P("layer", "row", "col"),
        P("row", "layer", "col"),
        P("layer", "row", "col"),
        P("row", ("col", "layer")),
    )
    small = mesh.shape["row"] == 4 and mesh.shape["col"] == 4 and mesh.shape["layer"] == 2
    return jax.shard_map(
        on_device if small else on_any_device,
        mesh=mesh,
        in_specs=placed,
        out_specs=P("row", ("col", "layer")),
        check_vma=False,
    )
```

```python
import functools

import jax
import jax.numpy as jnp
from jax import lax
from jax.experimental import pallas as pl
from jax.experimental.pallas import tpu as pltpu
from jax.sharding import PartitionSpec as P

epsilon = 1e-06
VMEM = pl.BlockSpec(memory_space=pltpu.VMEM)
room = pltpu.CompilerParams(vmem_limit_bytes=4 << 20)


def entry(mask, i, j):
    return mask[i : i + 1, j : j + 1] != 0


def keep_tiles(mask, turned, block, out):
    tall, wide = mask.shape[::-1] if turned else mask.shape
    high, broad = block.shape[0] // tall, block.shape[1] // wide
    for i in range(tall):
        for j in range(wide):
            at = (slice(i * high, (i + 1) * high), slice(j * broad, (j + 1) * broad))
            values = block[at]
            one = entry(mask, j, i) if turned else entry(mask, i, j)
            kept = jnp.broadcast_to(one, values.shape)
            out[at] = jnp.where(kept, values, jnp.zeros_like(values))


def tiles_kernel(*refs):
    operands, (right, left), held, arrived = refs[:4], refs[4:6], refs[6:10], refs[10]
    copies = []
    for n in range(4):
        parts = 1 if n % 2 == 0 else 4
        tall = operands[n].shape[0] // parts
        for part in range(parts):
            at = pl.ds(part * tall, tall)
            copy = pltpu.make_async_copy(
                operands[n].at[at], held[n].at[at], arrived.at[len(copies)]
            )
            copy.start()
            copies.append(copy)
    for copy in copies[:5]:
        copy.wait()
    keep_tiles(held[0], False, held[1], right)
    for copy in copies[5:]:
        copy.wait()
    keep_tiles(held[2], True, held[3], left)


def tiles(*operands):
    held = [pltpu.VMEM(value.shape, value.dtype) for value in operands]
    return pl.pallas_call(
        tiles_kernel,
        out_shape=[
            jax.ShapeDtypeStruct(operands[n].shape, operands[n].dtype) for n in (1, 3)
        ],
        in_specs=[pl.BlockSpec(memory_space=pltpu.HBM)] * 4,
        out_specs=[VMEM, VMEM],
        scratch_shapes=held + [pltpu.SemaphoreType.DMA((10,))],
        compiler_params=room,
        name="tiles",
    )(*(pltpu.with_memory_space_constraint(value, pltpu.HBM) for value in operands))


def call(kernel, name, shapes, *operands, scratch=()):
    return pl.pallas_call(
        kernel,
        out_shape=shapes,
        in_specs=[VMEM] * len(operands),
        out_specs=jax.tree.map(lambda _: VMEM, shapes),
        scratch_shapes=scratch,
        compiler_params=room,
        name=name,
    )(*operands)


def swapped(value, axis, step):
    count = lax.axis_size(axis)
    return lax.ppermute(value, axis, [(i, i ^ step) for i in range(count)])


def pair_kernel(here, beside, out):
    out[0] = here[...]
    out[1] = beside[...]


def early_kernel(near, far, right, first, second, inner, mask, out, left, held):
    held[0:2] = near[...]
    held[2:4] = far[...]
    row, col = lax.axis_index("row"), lax.axis_index("col")
    block = lax.rem(2 * row + 1, 5)
    left[...] = held[row ^ 3 ^ col]
    rows, columns = left.shape[0], out.shape[1]
    total = jnp.zeros((rows, columns), jnp.float32)
    for here, values in ((row, right), (block, first), (block ^ 3, second)):
        total += jnp.dot(
            held[here ^ col], values[...], preferred_element_type=jnp.float32
        )
    out[0:rows, :] = total

    @pl.when(jnp.logical_or(row == 1, row == 2))
    def _():
        out[0:rows, :] += jnp.dot(
            left[...], inner[...], preferred_element_type=jnp.float32
        )

    tall, wide = mask.shape
    broad = columns // 2 // wide
    for i in range(tall):
        for j in range(2 * wide):
            kept = entry(mask, i, j % wide).astype(jnp.float32)
            at = (slice(rows + i, rows + i + 1), slice(j * broad, (j + 1) * broad))
            out[at] = jnp.broadcast_to(kept, (1, broad))


def product_kernel(early, left, outer, out):
    row = lax.axis_index("row")
    rows = left.shape[0]
    out[...] = early[...]

    @pl.when(jnp.logical_or(row == 0, row == 3))
    def _():
        out[0:rows, :] += jnp.dot(
            left[...], outer[...], preferred_element_type=jnp.float32
        )


def inflate(own, side, rows, tall, wide, mine, got, out, sums):
    half = mine.shape[1] // 2
    broad = half // wide
    for j in range(wide):
        columns = slice(side * half + j * broad, side * half + (j + 1) * broad)
        total = jnp.zeros((1, broad), jnp.float32)
        for i in range(tall):
            high = rows // tall
            at = (slice(i * high, (i + 1) * high), columns)
            product = mine[at] + got[at]
            kept = (mine if own else got)[rows + i : rows + i + 1, columns] != 0.0
            value = jnp.where(jnp.broadcast_to(kept, product.shape), product * product, 0.0)
            if out is not None:
                out[at[0], j * broad : (j + 1) * broad] = value
            if sums is not None:
                total += jnp.sum(value, axis=0, keepdims=True)
        if sums is not None:
            sums[:, columns] = total


def sums_kernel(rows, tall, wide, mine, got, sums):
    sums[...] = jnp.zeros_like(sums)

    @pl.when(lax.axis_index("layer") == 1)
    def _():
        inflate(False, 0, rows, tall, wide, mine, got, None, sums)
        inflate(True, 1, rows, tall, wide, mine, got, None, sums)


def inflate_kernel(rows, tall, wide, mine, got, out, sums):
    sums[...] = jnp.zeros_like(sums)

    @pl.when(lax.axis_index("layer") == 0)
    def _():
        inflate(True, 0, rows, tall, wide, mine, got, out, sums)
        inflate(False, 1, rows, tall, wide, mine, got, None, sums)

    @pl.when(lax.axis_index("layer") == 1)
    def _():
        inflate(True, 1, rows, tall, wide, mine, got, out, None)


def on_device(left_blocks, batch_blocks, left_mask, batch_mask, prune_mask):
    f32 = jnp.float32
    rows, columns = left_blocks.shape[0], batch_blocks.shape[2]
    half = columns // 2
    right, left = tiles(
        batch_mask[0],
        batch_blocks[0],
        jnp.transpose(left_mask, (1, 2, 0))[0],
        left_blocks[:, 0, :],
    )
    count = lax.axis_size("row")
    first = lax.ppermute(right, "row", [(0, 2), (3, 1), (1, 0), (2, 3)])
    second = lax.ppermute(right, "row", [(0, 1), (3, 2), (1, 3), (2, 0)])
    pairs = [(2, 4), (3, 5), (4, 2), (5, 3), (0, 1), (1, 0), (6, 7), (7, 6)]
    inner = lax.ppermute(right, ("row", "layer"), pairs)
    outer = lax.ppermute(first, "row", [(0, 1), (1, 0), (2, 3), (3, 2)])
    beside = swapped(left, "col", 1)
    pair = call(
        pair_kernel, "pair", jax.ShapeDtypeStruct((2,) + left.shape, left.dtype), left, beside
    )
    piece = jax.ShapeDtypeStruct((rows, half), f32)
    tall, wide = prune_mask.shape
    whole = jax.ShapeDtypeStruct((rows + (tall + 7) // 8 * 8, columns), f32)
    early, last = call(
        early_kernel,
        "early",
        [whole, jax.ShapeDtypeStruct(left.shape, left.dtype)],
        pair,
        swapped(pair, "col", 2),
        right,
        first,
        second,
        inner,
        prune_mask,
        scratch=[pltpu.VMEM((4,) + left.shape, left.dtype)],
    )
    partial = call(product_kernel, "product", whole, early, last, outer)
    got = swapped(partial, "layer", 1)
    line = jax.ShapeDtypeStruct((1, columns), f32)
    sums = call(
        functools.partial(sums_kernel, rows, tall, wide), "sums", line, partial, got
    )
    inflated, sums_here = call(
        functools.partial(inflate_kernel, rows, tall, wide),
        "inflate",
        [piece, line],
        partial,
        got,
    )
    steps = [(2 * z + 1, 2 * (z ^ 1)) for z in range(4)] + [(2 * z, 2 * z + 1) for z in range(4)]
    sums = sums_here + lax.ppermute(sums, ("row", "layer"), steps)
    steps = [(2 * z, 2 * (z ^ 2) + 1) for z in range(4)] + [(2 * z + 1, 2 * z) for z in range(4)]
    far = lax.ppermute(sums, ("row", "layer"), steps)
    low = lax.axis_index("layer") == 0
    half_sums = jnp.where(low, sums, far)
    total = half_sums + swapped(half_sums, "layer", 1)
    sums = jnp.where(low, total[:, :half], total[:, half:])
    total_rows = rows * count
    return inflated * (total_rows / (sums + epsilon))


def widen(mask, tile_size, dtype):
    first, last = mask.shape
    spread = jnp.broadcast_to(
        mask.astype(dtype)[:, None, :, None], (first, tile_size, last, tile_size)
    )
    return spread.reshape(first * tile_size, last * tile_size)


def on_any_device(left_blocks, batch_blocks, left_mask, batch_mask, prune_mask):
    tile_size = left_blocks.shape[0] // left_mask.shape[0]
    left = left_blocks[:, 0, :] * widen(left_mask[:, 0, :], tile_size, jnp.bfloat16)
    right = batch_blocks[0] * widen(batch_mask[0], tile_size, jnp.bfloat16)
    product = jnp.dot(
        lax.all_gather(left, "col", axis=1, tiled=True),
        lax.all_gather(right, "row", axis=0, tiled=True),
        preferred_element_type=jnp.float32,
    )
    own_share = lax.psum_scatter(product, "layer", scatter_dimension=1, tiled=True)
    inflated = own_share * own_share * widen(prune_mask, tile_size, jnp.float32)
    col_sums = lax.psum(jnp.sum(inflated, axis=0), "row")
    total_rows = left.shape[0] * lax.axis_size("row")
    return inflated * (total_rows / (col_sums + epsilon))


def solution(mesh):
    placed = (
        P("row", "layer", "col"),
        P("layer", "row", "col"),
        P("row", "layer", "col"),
        P("layer", "row", "col"),
        P("row", ("col", "layer")),
    )
    small = mesh.shape["row"] == 4 and mesh.shape["col"] == 4 and mesh.shape["layer"] == 2
    return jax.shard_map(
        on_device if small else on_any_device,
        mesh=mesh,
        in_specs=placed,
        out_specs=P("row", ("col", "layer")),
        check_vma=False,
    )
```

```python
import functools

import jax
import jax.numpy as jnp
from jax import lax
from jax.experimental import pallas as pl
from jax.experimental.pallas import tpu as pltpu
from jax.sharding import PartitionSpec as P

epsilon = 1e-06
VMEM = pl.BlockSpec(memory_space=pltpu.VMEM)
room = pltpu.CompilerParams(vmem_limit_bytes=4 << 20)


def entry(mask, i, j):
    return mask[i : i + 1, j : j + 1] != 0


def keep_tiles(mask, turned, block, out):
    tall, wide = mask.shape[::-1] if turned else mask.shape
    high, broad = block.shape[0] // tall, block.shape[1] // wide
    for i in range(tall):
        for j in range(wide):
            at = (slice(i * high, (i + 1) * high), slice(j * broad, (j + 1) * broad))
            values = block[at]
            one = entry(mask, j, i) if turned else entry(mask, i, j)
            kept = jnp.broadcast_to(one, values.shape)
            out[at] = jnp.where(kept, values, jnp.zeros_like(values))


def tiles_kernel(*refs):
    operands, (right, left), held, arrived = refs[:4], refs[4:6], refs[6:10], refs[10]
    copies = []
    for n in range(4):
        parts = 1 if n % 2 == 0 else 4
        tall = operands[n].shape[0] // parts
        for part in range(parts):
            at = pl.ds(part * tall, tall)
            copy = pltpu.make_async_copy(
                operands[n].at[at], held[n].at[at], arrived.at[len(copies)]
            )
            copy.start()
            copies.append(copy)
    for copy in copies[:5]:
        copy.wait()
    keep_tiles(held[0], False, held[1], right)
    for copy in copies[5:]:
        copy.wait()
    keep_tiles(held[2], True, held[3], left)


def tiles(*operands):
    held = [pltpu.VMEM(value.shape, value.dtype) for value in operands]
    return pl.pallas_call(
        tiles_kernel,
        out_shape=[
            jax.ShapeDtypeStruct(operands[n].shape, operands[n].dtype) for n in (1, 3)
        ],
        in_specs=[pl.BlockSpec(memory_space=pltpu.HBM)] * 4,
        out_specs=[VMEM, VMEM],
        scratch_shapes=held + [pltpu.SemaphoreType.DMA((10,))],
        compiler_params=room,
        name="tiles",
    )(*(pltpu.with_memory_space_constraint(value, pltpu.HBM) for value in operands))


def call(kernel, name, shapes, *operands, scratch=()):
    return pl.pallas_call(
        kernel,
        out_shape=shapes,
        in_specs=[VMEM] * len(operands),
        out_specs=jax.tree.map(lambda _: VMEM, shapes),
        scratch_shapes=scratch,
        compiler_params=room,
        name=name,
    )(*operands)


def swapped(value, axis, step):
    count = lax.axis_size(axis)
    return lax.ppermute(value, axis, [(i, i ^ step) for i in range(count)])


def pair_kernel(here, beside, out):
    out[0] = here[...]
    out[1] = beside[...]


def early_kernel(near, far, right, first, second, inner, mask, *refs):
    outs, left, handed, held = refs[:-3], refs[-3], refs[-2], refs[-1]
    handed[...] = inner[...]
    held[0:2] = near[...]
    held[2:4] = far[...]
    row, col = lax.axis_index("row"), lax.axis_index("col")
    block = lax.rem(2 * row + 1, 5)
    left[...] = held[row ^ 3 ^ col]
    (rows, depth), broad = left.shape, outs[0].shape[1]
    tall, wide = mask.shape
    share = rows // len(outs)
    for n, out in enumerate(outs):
        columns = slice(n * broad, (n + 1) * broad)
        total = jnp.zeros((rows, broad), jnp.float32)
        for here, values in ((row, right), (block, first), (block ^ 3, second)):
            total += jnp.dot(
                held[here ^ col], values[:, columns], preferred_element_type=jnp.float32
            )
        out[0:rows, :] = total
        for i in range(tall):
            kept = entry(mask, i, n % wide).astype(jnp.float32)
            out[rows + i : rows + i + 1, :] = jnp.broadcast_to(kept, (1, broad))
        out[out.shape[0] - share :, :] = left[n * share : (n + 1) * share, :].astype(
            jnp.float32
        )


def last_kernel(inner, outer, out):
    row = lax.axis_index("row")

    @pl.when(jnp.logical_or(row == 1, row == 2))
    def _():
        out[...] = inner[...]

    @pl.when(jnp.logical_or(row == 0, row == 3))
    def _():
        out[...] = outer[...]


def inflate(own, sides, sizes, ours, theirs, out, sums):
    rows, half, tall, wide = sizes
    high, broad = rows // tall, half // wide
    share = rows // (2 * wide)
    here = ours[-2][...]
    there = jnp.concatenate([part[part.shape[0] - share :, :] for part in theirs[:-1]], axis=0)
    left = jnp.concatenate([here, there.astype(here.dtype)], axis=1)
    for n in range(2 * wide):
        if n // wide not in sides:
            continue
        columns = slice(n * broad, (n + 1) * broad)
        right = jnp.concatenate([ours[-1][:, columns], theirs[-1][:, columns]], axis=0)
        product = ours[n][0:rows, :] + theirs[n][0:rows, :]
        product += jnp.dot(left, right, preferred_element_type=jnp.float32)
        total = jnp.zeros((1, broad), jnp.float32)
        across = slice(n % wide * broad, (n % wide + 1) * broad)
        for i in range(tall):
            at = slice(i * high, (i + 1) * high)
            kept = (ours if n // wide == own else theirs)[n][rows + i : rows + i + 1, :] != 0.0
            kept = jnp.broadcast_to(kept, (high, broad))
            value = jnp.where(kept, product[at, :] * product[at, :], 0.0)
            if n // wide == own and out is not None:
                out[at, across] = value
            total += jnp.sum(value, axis=0, keepdims=True)
        if sums is not None:
            sums[:, columns] = total


def sums_kernel(sizes, *refs):
    count = 2 * sizes[3]
    ours, theirs, sums = refs[: count + 2], refs[count + 2 : -1], refs[-1]
    sums[...] = jnp.zeros_like(sums)

    @pl.when(lax.axis_index("layer") == 1)
    def _():
        inflate(1, (0, 1), sizes, ours, theirs, None, sums)


def inflate_kernel(sizes, *refs):
    count = 2 * sizes[3]
    ours, theirs, out, sums = refs[: count + 2], refs[count + 2 : -2], refs[-2], refs[-1]
    sums[...] = jnp.zeros_like(sums)

    @pl.when(lax.axis_index("layer") == 0)
    def _():
        inflate(0, (0, 1), sizes, ours, theirs, out, sums)

    @pl.when(lax.axis_index("layer") == 1)
    def _():
        inflate(1, (1,), sizes, ours, theirs, out, None)


def on_device(left_blocks, batch_blocks, left_mask, batch_mask, prune_mask):
    f32 = jnp.float32
    rows, columns = left_blocks.shape[0], batch_blocks.shape[2]
    half = columns // 2
    right, left = tiles(
        batch_mask[0],
        batch_blocks[0],
        jnp.transpose(left_mask, (1, 2, 0))[0],
        left_blocks[:, 0, :],
    )
    count = lax.axis_size("row")
    first = lax.ppermute(right, "row", [(0, 2), (3, 1), (1, 0), (2, 3)])
    second = lax.ppermute(right, "row", [(0, 1), (3, 2), (1, 3), (2, 0)])
    pairs = [(2, 4), (3, 5), (4, 2), (5, 3), (0, 1), (1, 0), (6, 7), (7, 6)]
    inner = lax.ppermute(right, ("row", "layer"), pairs)
    outer = lax.ppermute(first, "row", [(0, 1), (1, 0), (2, 3), (3, 2)])
    beside = swapped(left, "col", 1)
    pair = call(
        pair_kernel, "pair", jax.ShapeDtypeStruct((2,) + left.shape, left.dtype), left, beside
    )
    piece = jax.ShapeDtypeStruct((rows, half), f32)
    tall, wide = prune_mask.shape
    parts = 2 * wide
    share = rows // parts
    part = jax.ShapeDtypeStruct((rows + (tall + 7) // 8 * 8 + share, columns // parts), f32)
    ours = call(
        early_kernel,
        "early",
        [part] * parts + [jax.ShapeDtypeStruct(v.shape, v.dtype) for v in (left, right)],
        pair,
        swapped(pair, "col", 2),
        right,
        first,
        second,
        inner,
        prune_mask,
        scratch=[pltpu.VMEM((4,) + left.shape, left.dtype)],
    )
    last = call(
        last_kernel, "last", jax.ShapeDtypeStruct(right.shape, right.dtype), ours[-1], outer
    )
    operands = list(ours[:-1]) + [last]
    operands += [swapped(value, "layer", 1) for value in ours[:-2]]
    operands.append(swapped(last, "layer", 1))
    sizes = (rows, half, tall, wide)
    line = jax.ShapeDtypeStruct((1, columns), f32)
    sums = call(functools.partial(sums_kernel, sizes), "sums", line, *operands)
    inflated, sums_here = call(
        functools.partial(inflate_kernel, sizes), "inflate", [piece, line], *operands
    )
    total = sums_here
    for step in (1, 2, 3):
        pairs = [(2 * z + 1, 2 * (z ^ step)) for z in range(count)]
        pairs += [(2 * z, 2 * z + 1) for z in range(count)]
        total = total + lax.ppermute(sums, ("row", "layer"), pairs)
    low = lax.axis_index("layer") == 0
    sums = jnp.where(low, total[:, :half], swapped(total[:, half:], "layer", 1))
    total_rows = rows * count
    return inflated * (total_rows / (sums + epsilon))


def widen(mask, tile_size, dtype):
    first, last = mask.shape
    spread = jnp.broadcast_to(
        mask.astype(dtype)[:, None, :, None], (first, tile_size, last, tile_size)
    )
    return spread.reshape(first * tile_size, last * tile_size)


def on_any_device(left_blocks, batch_blocks, left_mask, batch_mask, prune_mask):
    tile_size = left_blocks.shape[0] // left_mask.shape[0]
    left = left_blocks[:, 0, :] * widen(left_mask[:, 0, :], tile_size, jnp.bfloat16)
    right = batch_blocks[0] * widen(batch_mask[0], tile_size, jnp.bfloat16)
    product = jnp.dot(
        lax.all_gather(left, "col", axis=1, tiled=True),
        lax.all_gather(right, "row", axis=0, tiled=True),
        preferred_element_type=jnp.float32,
    )
    own_share = lax.psum_scatter(product, "layer", scatter_dimension=1, tiled=True)
    inflated = own_share * own_share * widen(prune_mask, tile_size, jnp.float32)
    col_sums = lax.psum(jnp.sum(inflated, axis=0), "row")
    total_rows = left.shape[0] * lax.axis_size("row")
    return inflated * (total_rows / (col_sums + epsilon))


def solution(mesh):
    placed = (
        P("row", "layer", "col"),
        P("layer", "row", "col"),
        P("row", "layer", "col"),
        P("layer", "row", "col"),
        P("row", ("col", "layer")),
    )
    small = mesh.shape["row"] == 4 and mesh.shape["col"] == 4 and mesh.shape["layer"] == 2
    return jax.shard_map(
        on_device if small else on_any_device,
        mesh=mesh,
        in_specs=placed,
        out_specs=P("row", ("col", "layer")),
        check_vma=False,
    )
```

```python
import functools

import jax
import jax.numpy as jnp
from jax import lax
from jax.experimental import pallas as pl
from jax.experimental.pallas import tpu as pltpu
from jax.sharding import PartitionSpec as P

epsilon = 1e-06
VMEM = pl.BlockSpec(memory_space=pltpu.VMEM)
room = pltpu.CompilerParams(vmem_limit_bytes=4 << 20)


def entry(mask, i, j):
    return mask[i : i + 1, j : j + 1] != 0


def keep_tiles(mask, turned, block, out):
    tall, wide = mask.shape[::-1] if turned else mask.shape
    high, broad = block.shape[0] // tall, block.shape[1] // wide
    for i in range(tall):
        for j in range(wide):
            at = (slice(i * high, (i + 1) * high), slice(j * broad, (j + 1) * broad))
            values = block[at]
            one = entry(mask, j, i) if turned else entry(mask, i, j)
            kept = jnp.broadcast_to(one, values.shape)
            out[at] = jnp.where(kept, values, jnp.zeros_like(values))


def tiles_kernel(*refs):
    operands, (right, left, prune), held, arrived = refs[:5], refs[5:8], refs[8:12], refs[12]
    copies = []
    for n, target in enumerate(held + (prune,)):
        parts = 4 if n in (1, 3) else 1
        tall = operands[n].shape[0] // parts
        for part in range(parts):
            at = pl.ds(part * tall, tall)
            copy = pltpu.make_async_copy(
                operands[n].at[at], target.at[at], arrived.at[len(copies)]
            )
            copy.start()
            copies.append(copy)
    for copy in copies[:5]:
        copy.wait()
    keep_tiles(held[0], False, held[1], right)
    for copy in copies[5:]:
        copy.wait()
    keep_tiles(held[2], True, held[3], left)


def tiles(*operands):
    held = [pltpu.VMEM(value.shape, value.dtype) for value in operands[:4]]
    return pl.pallas_call(
        tiles_kernel,
        out_shape=[
            jax.ShapeDtypeStruct(operands[n].shape, operands[n].dtype) for n in (1, 3, 4)
        ],
        in_specs=[pl.BlockSpec(memory_space=pltpu.HBM)] * 5,
        out_specs=[VMEM, VMEM, VMEM],
        scratch_shapes=held + [pltpu.SemaphoreType.DMA((11,))],
        compiler_params=room,
        name="tiles",
    )(*(pltpu.with_memory_space_constraint(value, pltpu.HBM) for value in operands))


def call(kernel, name, shapes, *operands, scratch=()):
    return pl.pallas_call(
        kernel,
        out_shape=shapes,
        in_specs=[VMEM] * len(operands),
        out_specs=jax.tree.map(lambda _: VMEM, shapes),
        scratch_shapes=scratch,
        compiler_params=room,
        name=name,
    )(*operands)


def swapped(value, axis, step):
    count = lax.axis_size(axis)
    return lax.ppermute(value, axis, [(i, i ^ step) for i in range(count)])


def pair_kernel(here, beside, out):
    out[0] = here[...]
    out[1] = beside[...]


def stack_kernel(*refs):
    for n, block in enumerate(refs[:-1]):
        refs[-1][n] = block[...]


def hand_kernel(block, after, out):
    out[...] = block[...]


def early_kernel(near, far, rights, after, mask, *refs):
    outs, left, held = refs[:-2], refs[-2], refs[-1]
    held[0:2] = near[...]
    held[2:4] = far[...]
    row, col = lax.axis_index("row"), lax.axis_index("col")
    block = lax.rem(2 * row + 1, 5)
    left[...] = held[row ^ 3 ^ col]
    (rows, depth), broad = left.shape, outs[0].shape[1]
    tall, wide = mask.shape
    share = rows // len(outs)
    lefts = [held[here ^ col] for here in (row, block, block ^ 3)]
    total = jnp.dot(
        jnp.concatenate(lefts, axis=1),
        rights[...].reshape(3 * depth, -1),
        preferred_element_type=jnp.float32,
    )
    for n, out in enumerate(outs):
        out[0:rows, :] = total[:, n * broad : (n + 1) * broad]
        for i in range(tall):
            kept = entry(mask, i, n % wide).astype(jnp.float32)
            out[rows + i : rows + i + 1, :] = jnp.broadcast_to(kept, (1, broad))
        out[out.shape[0] - share :, :] = left[n * share : (n + 1) * share, :].astype(
            jnp.float32
        )


def last_kernel(inner, outer, out):
    row = lax.axis_index("row")

    @pl.when(jnp.logical_or(row == 1, row == 2))
    def _():
        out[...] = inner[...]

    @pl.when(jnp.logical_or(row == 0, row == 3))
    def _():
        out[...] = outer[...]


def inflate(own, sides, sizes, ours, theirs, out, sums):
    rows, half, tall, wide = sizes
    high, broad = rows // tall, half // wide
    share = rows // (2 * wide)
    here = ours[-2][...]
    there = jnp.concatenate([part[part.shape[0] - share :, :] for part in theirs[:-1]], axis=0)
    left = jnp.concatenate([here, there.astype(here.dtype)], axis=1)
    for n in range(2 * wide):
        if n // wide not in sides:
            continue
        columns = slice(n * broad, (n + 1) * broad)
        right = jnp.concatenate([ours[-1][:, columns], theirs[-1][:, columns]], axis=0)
        product = ours[n][0:rows, :] + theirs[n][0:rows, :]
        product += jnp.dot(left, right, preferred_element_type=jnp.float32)
        total = jnp.zeros((1, broad), jnp.float32)
        across = slice(n % wide * broad, (n % wide + 1) * broad)
        for i in range(tall):
            at = slice(i * high, (i + 1) * high)
            kept = (ours if n // wide == own else theirs)[n][rows + i : rows + i + 1, :] != 0.0
            kept = jnp.broadcast_to(kept, (high, broad))
            value = jnp.where(kept, product[at, :] * product[at, :], 0.0)
            if n // wide == own and out is not None:
                out[at, across] = value
            total += jnp.sum(value, axis=0, keepdims=True)
        if sums is not None:
            sums[:, columns] = total


def sums_kernel(sizes, *refs):
    count = 2 * sizes[3]
    ours, theirs, sums = refs[: count + 2], refs[count + 2 : -1], refs[-1]
    sums[...] = jnp.zeros_like(sums)

    @pl.when(lax.axis_index("layer") == 1)
    def _():
        inflate(1, (0, 1), sizes, ours, theirs, None, sums)


def inflate_kernel(sizes, *refs):
    count = 2 * sizes[3]
    ours, theirs, out, sums = refs[: count + 2], refs[count + 2 : -2], refs[-2], refs[-1]
    sums[...] = jnp.zeros_like(sums)

    @pl.when(lax.axis_index("layer") == 0)
    def _():
        inflate(0, (0, 1), sizes, ours, theirs, out, sums)

    @pl.when(lax.axis_index("layer") == 1)
    def _():
        inflate(1, (1,), sizes, ours, theirs, out, None)


def scale_kernel(turn, total_rows, inflated, sums, *refs):
    out, scaled, sent = refs[-3:]
    rows = inflated.shape[0]
    parts = sent.shape[0]

    @pl.when(lax.axis_index("layer") == turn)
    def _():
        scale = total_rows / (sums[...] + epsilon)
        copies = []
        for part in range(parts):
            at = pl.ds(part * (rows // parts), rows // parts)
            scaled[at, :] = inflated[at, :] * scale
            copies.append(pltpu.make_async_copy(scaled.at[at], out.at[at], sent.at[part]))
            copies[-1].start()
        for copy in copies:
            copy.wait()


def scaled_on(turn, total_rows, inflated, sums, before=()):
    hbm = pl.BlockSpec(memory_space=pltpu.HBM)
    size = inflated.size
    return pl.pallas_call(
        functools.partial(scale_kernel, turn, total_rows),
        out_shape=jax.ShapeDtypeStruct(inflated.shape, inflated.dtype),
        in_specs=[VMEM, VMEM] + [hbm] * len(before),
        out_specs=hbm,
        scratch_shapes=[
            pltpu.VMEM(inflated.shape, inflated.dtype),
            pltpu.SemaphoreType.DMA((2,)),
        ],
        input_output_aliases={2: 0} if before else {},
        cost_estimate=pl.CostEstimate(flops=size, bytes_accessed=8 * size, transcendentals=0),
        compiler_params=room,
        name=f"scale_{turn}",
    )(inflated, sums, *before)


def on_device(left_blocks, batch_blocks, left_mask, batch_mask, prune_mask):
    f32 = jnp.float32
    rows, columns = left_blocks.shape[0], batch_blocks.shape[2]
    half = columns // 2
    right, left, prune_mask = tiles(
        batch_mask[0],
        batch_blocks[0],
        jnp.transpose(left_mask, (1, 2, 0))[0],
        left_blocks[:, 0, :],
        prune_mask,
    )
    count = lax.axis_size("row")
    first = lax.ppermute(right, "row", [(0, 2), (3, 1), (1, 0), (2, 3)])
    second = lax.ppermute(right, "row", [(0, 1), (3, 2), (1, 3), (2, 0)])
    pairs = [(2, 4), (3, 5), (4, 2), (5, 3), (0, 1), (1, 0), (6, 7), (7, 6)]
    inner = lax.ppermute(right, ("row", "layer"), pairs)
    outer = lax.ppermute(first, "row", [(0, 1), (1, 0), (2, 3), (3, 2)])
    beside = swapped(left, "col", 1)
    pair = call(
        pair_kernel, "pair", jax.ShapeDtypeStruct((2,) + left.shape, left.dtype), left, beside
    )
    piece = jax.ShapeDtypeStruct((rows, half), f32)
    tall, wide = prune_mask.shape
    parts = 2 * wide
    share = rows // parts
    part = jax.ShapeDtypeStruct((rows + (tall + 7) // 8 * 8 + share, columns // parts), f32)
    block = jax.ShapeDtypeStruct(right.shape, right.dtype)
    rights = jax.ShapeDtypeStruct((3,) + right.shape, right.dtype)
    rights = call(stack_kernel, "rights", rights, right, first, second)
    handed = call(hand_kernel, "inner", block, inner, rights)
    ours = call(
        early_kernel,
        "early",
        [part] * parts + [jax.ShapeDtypeStruct(left.shape, left.dtype)],
        pair,
        swapped(pair, "col", 2),
        rights,
        handed,
        prune_mask,
        scratch=[pltpu.VMEM((4,) + left.shape, left.dtype)],
    )
    last = call(
        last_kernel, "last", block, handed, outer
    )
    operands = list(ours) + [last]
    operands += [swapped(value, "layer", 1) for value in ours[:-1]]
    operands.append(swapped(last, "layer", 1))
    sizes = (rows, half, tall, wide)
    line = jax.ShapeDtypeStruct((1, columns), f32)
    sums = call(functools.partial(sums_kernel, sizes), "sums", line, *operands)
    inflated, sums_here = call(
        functools.partial(inflate_kernel, sizes), "inflate", [piece, line], *operands
    )
    total = sums_here
    for step in (1, 2, 3):
        pairs = [(2 * z + 1, 2 * (z ^ step)) for z in range(count)]
        pairs += [(2 * z, 2 * z + 1) for z in range(count)]
        total = total + lax.ppermute(sums, ("row", "layer"), pairs)
    total_rows = rows * count
    scaled = scaled_on(0, total_rows, inflated, total[:, :half])
    total_high = swapped(total[:, half:], "layer", 1)
    return scaled_on(1, total_rows, inflated, total_high, (scaled,))


def widen(mask, tile_size, dtype):
    first, last = mask.shape
    spread = jnp.broadcast_to(
        mask.astype(dtype)[:, None, :, None], (first, tile_size, last, tile_size)
    )
    return spread.reshape(first * tile_size, last * tile_size)


def on_any_device(left_blocks, batch_blocks, left_mask, batch_mask, prune_mask):
    tile_size = left_blocks.shape[0] // left_mask.shape[0]
    left = left_blocks[:, 0, :] * widen(left_mask[:, 0, :], tile_size, jnp.bfloat16)
    right = batch_blocks[0] * widen(batch_mask[0], tile_size, jnp.bfloat16)
    product = jnp.dot(
        lax.all_gather(left, "col", axis=1, tiled=True),
        lax.all_gather(right, "row", axis=0, tiled=True),
        preferred_element_type=jnp.float32,
    )
    own_share = lax.psum_scatter(product, "layer", scatter_dimension=1, tiled=True)
    inflated = own_share * own_share * widen(prune_mask, tile_size, jnp.float32)
    col_sums = lax.psum(jnp.sum(inflated, axis=0), "row")
    total_rows = left.shape[0] * lax.axis_size("row")
    return inflated * (total_rows / (col_sums + epsilon))


def solution(mesh):
    placed = (
        P("row", "layer", "col"),
        P("layer", "row", "col"),
        P("row", "layer", "col"),
        P("layer", "row", "col"),
        P("row", ("col", "layer")),
    )
    small = mesh.shape["row"] == 4 and mesh.shape["col"] == 4 and mesh.shape["layer"] == 2
    return jax.shard_map(
        on_device if small else on_any_device,
        mesh=mesh,
        in_specs=placed,
        out_specs=P("row", ("col", "layer")),
        check_vma=False,
    )
```

```python
import functools

import jax
import jax.numpy as jnp
from jax import lax
from jax.experimental import pallas as pl
from jax.experimental.pallas import tpu as pltpu
from jax.sharding import PartitionSpec as P

epsilon = 1e-06
VMEM = pl.BlockSpec(memory_space=pltpu.VMEM)
room = pltpu.CompilerParams(vmem_limit_bytes=4 << 20)


def entry(mask, i, j):
    return mask[i : i + 1, j : j + 1] != 0


def keep_tiles(mask, turned, block, out):
    tall, wide = mask.shape[::-1] if turned else mask.shape
    high, broad = block.shape[0] // tall, block.shape[1] // wide
    for i in range(tall):
        for j in range(wide):
            at = (slice(i * high, (i + 1) * high), slice(j * broad, (j + 1) * broad))
            values = block[at]
            one = entry(mask, j, i) if turned else entry(mask, i, j)
            kept = jnp.broadcast_to(one, values.shape)
            out[at] = jnp.where(kept, values, jnp.zeros_like(values))


def tiles_kernel(*refs):
    operands, (right, left, prune), held, arrived = refs[:5], refs[5:8], refs[8:12], refs[12]
    copies = []
    for n, target in enumerate(held + (prune,)):
        parts = 4 if n in (1, 3) else 1
        tall = operands[n].shape[0] // parts
        for part in range(parts):
            at = pl.ds(part * tall, tall)
            copy = pltpu.make_async_copy(
                operands[n].at[at], target.at[at], arrived.at[len(copies)]
            )
            copy.start()
            copies.append(copy)
    for copy in copies[:5]:
        copy.wait()
    keep_tiles(held[0], False, held[1], right)
    for copy in copies[5:]:
        copy.wait()
    keep_tiles(held[2], True, held[3], left)


def tiles(*operands):
    held = [pltpu.VMEM(value.shape, value.dtype) for value in operands[:4]]
    return pl.pallas_call(
        tiles_kernel,
        out_shape=[
            jax.ShapeDtypeStruct(operands[n].shape, operands[n].dtype) for n in (1, 3, 4)
        ],
        in_specs=[pl.BlockSpec(memory_space=pltpu.HBM)] * 5,
        out_specs=[VMEM, VMEM, VMEM],
        scratch_shapes=held + [pltpu.SemaphoreType.DMA((11,))],
        compiler_params=room,
        name="tiles",
    )(*(pltpu.with_memory_space_constraint(value, pltpu.HBM) for value in operands))


def call(kernel, name, shapes, *operands, scratch=()):
    return pl.pallas_call(
        kernel,
        out_shape=shapes,
        in_specs=[VMEM] * len(operands),
        out_specs=jax.tree.map(lambda _: VMEM, shapes),
        scratch_shapes=scratch,
        compiler_params=room,
        name=name,
    )(*operands)


def swapped(value, axis, step):
    count = lax.axis_size(axis)
    return lax.ppermute(value, axis, [(i, i ^ step) for i in range(count)])


def pair_kernel(here, beside, out):
    out[0] = here[...]
    out[1] = beside[...]


def stack_kernel(*refs):
    for n, block in enumerate(refs[:-1]):
        refs[-1][n] = block[...]


def hand_kernel(block, after, out):
    out[...] = block[...]


def early_kernel(near, far, rights, after, mask, *refs):
    outs, left, held = refs[:-2], refs[-2], refs[-1]
    held[0:2] = near[...]
    held[2:4] = far[...]
    row, col = lax.axis_index("row"), lax.axis_index("col")
    block = lax.rem(2 * row + 1, 5)
    left[...] = held[row ^ 3 ^ col]
    (rows, depth), broad = left.shape, outs[0].shape[1]
    tall, wide = mask.shape
    share = rows // len(outs)
    lefts = [held[here ^ col] for here in (row, block, block ^ 3)]
    total = jnp.dot(
        jnp.concatenate(lefts, axis=1),
        rights[...].reshape(3 * depth, -1),
        preferred_element_type=jnp.float32,
    )
    for n, out in enumerate(outs):
        out[0:rows, :] = total[:, n * broad : (n + 1) * broad]
        out[rows : out.shape[0] - share, :] = jnp.zeros_like(
            out[rows : out.shape[0] - share, :]
        )
        for i in range(tall):
            kept = entry(mask, i, n % wide).astype(jnp.float32)
            out[rows + i : rows + i + 1, :] = jnp.broadcast_to(kept, (1, broad))
        out[out.shape[0] - share :, :] = left[n * share : (n + 1) * share, :].astype(
            jnp.float32
        )


def last_kernel(inner, outer, out):
    row = lax.axis_index("row")

    @pl.when(jnp.logical_or(row == 1, row == 2))
    def _():
        out[...] = inner[...]

    @pl.when(jnp.logical_or(row == 0, row == 3))
    def _():
        out[...] = outer[...]


def join_kernel(sizes, *refs):
    rows, half, tall, wide = sizes
    count = 2 * wide
    ours, left, theirs = refs[:count], refs[count], refs[count + 1 : -3]
    total, kept, lefts = refs[-3:]
    broad = half // wide
    share = rows // count
    depth = left.shape[1]
    layer = lax.axis_index("layer")
    lefts[:, 0:depth] = left[...]
    for n in range(count):
        columns = slice(n * broad, (n + 1) * broad)
        total[:, columns] = ours[n][0:rows, :] + theirs[n][0:rows, :]
        entries = slice(rows, rows + kept.shape[0])
        own = layer == n // wide
        kept[:, columns] = jnp.where(own, ours[n][entries, :], theirs[n][entries, :])
        lefts[n * share : (n + 1) * share, depth:] = theirs[n][
            theirs[n].shape[0] - share :, :
        ].astype(left.dtype)


def inflate(side, sizes, joined, out, sums):
    rows, half, tall, wide = sizes
    early, kept, lefts, here, there = joined
    high = rows // tall
    columns = slice(side * half, (side + 1) * half)
    product = early[:, columns] + jnp.dot(
        lefts[...],
        jnp.concatenate([here[:, columns], there[:, columns]], axis=0),
        preferred_element_type=jnp.float32,
    )
    total = jnp.zeros((1, half), jnp.float32)
    for i in range(tall):
        at = slice(i * high, (i + 1) * high)
        keep = jnp.broadcast_to(kept[i : i + 1, columns] != 0.0, (high, half))
        value = jnp.where(keep, product[at, :] * product[at, :], 0.0)
        if out is not None:
            out[at, :] = value
        total += jnp.sum(value, axis=0, keepdims=True)
    sums[...] = total


def sums_kernel(sizes, *refs):
    for core in range(2):

        @pl.when(lax.axis_index("layer") == core)
        def _():
            inflate(1 - core, sizes, refs[:-1], None, refs[-1])


def inflate_kernel(sizes, *refs):
    for core in range(2):

        @pl.when(lax.axis_index("layer") == core)
        def _():
            inflate(core, sizes, refs[:-2], refs[-2], refs[-1])


def on_device(left_blocks, batch_blocks, left_mask, batch_mask, prune_mask):
    f32 = jnp.float32
    rows, columns = left_blocks.shape[0], batch_blocks.shape[2]
    half = columns // 2
    right, left, prune_mask = tiles(
        batch_mask[0],
        batch_blocks[0],
        jnp.transpose(left_mask, (1, 2, 0))[0],
        left_blocks[:, 0, :],
        prune_mask,
    )
    count = lax.axis_size("row")
    first = lax.ppermute(right, "row", [(0, 2), (3, 1), (1, 0), (2, 3)])
    second = lax.ppermute(right, "row", [(0, 1), (3, 2), (1, 3), (2, 0)])
    pairs = [(2, 4), (3, 5), (4, 2), (5, 3), (0, 1), (1, 0), (6, 7), (7, 6)]
    inner = lax.ppermute(right, ("row", "layer"), pairs)
    outer = lax.ppermute(first, "row", [(0, 1), (1, 0), (2, 3), (3, 2)])
    beside = swapped(left, "col", 1)
    pair = call(
        pair_kernel, "pair", jax.ShapeDtypeStruct((2,) + left.shape, left.dtype), left, beside
    )
    piece = jax.ShapeDtypeStruct((rows, half), f32)
    tall, wide = prune_mask.shape
    parts = 2 * wide
    share = rows // parts
    part = jax.ShapeDtypeStruct((rows + (tall + 7) // 8 * 8 + share, columns // parts), f32)
    block = jax.ShapeDtypeStruct(right.shape, right.dtype)
    rights = jax.ShapeDtypeStruct((3,) + right.shape, right.dtype)
    rights = call(stack_kernel, "rights", rights, right, first, second)
    handed = call(hand_kernel, "inner", block, inner, rights)
    ours = call(
        early_kernel,
        "early",
        [part] * parts + [jax.ShapeDtypeStruct(left.shape, left.dtype)],
        pair,
        swapped(pair, "col", 2),
        rights,
        handed,
        prune_mask,
        scratch=[pltpu.VMEM((4,) + left.shape, left.dtype)],
    )
    last = call(
        last_kernel, "last", block, handed, outer
    )
    sizes = (rows, half, tall, wide)
    operands = list(call(
        functools.partial(join_kernel, sizes),
        "join",
        [
            jax.ShapeDtypeStruct((rows, columns), f32),
            jax.ShapeDtypeStruct(((tall + 7) // 8 * 8, columns), f32),
            jax.ShapeDtypeStruct((rows, 2 * left.shape[1]), left.dtype),
        ],
        *ours,
        *(swapped(value, "layer", 1) for value in ours[:-1]),
    ))
    operands += [last, swapped(last, "layer", 1)]
    line = jax.ShapeDtypeStruct((1, half), f32)
    sums = call(functools.partial(sums_kernel, sizes), "sums", line, *operands)
    inflated, sums_here = call(
        functools.partial(inflate_kernel, sizes), "inflate", [piece, line], *operands
    )
    total = sums_here
    for step in (1, 2, 3):
        pairs = [
            (2 * z + core, 2 * (z ^ step) + 1 - core)
            for z in range(count)
            for core in range(2)
        ]
        total = total + lax.ppermute(sums, ("row", "layer"), pairs)
    return inflated * (rows * count / (total + epsilon))


def widen(mask, tile_size, dtype):
    first, last = mask.shape
    spread = jnp.broadcast_to(
        mask.astype(dtype)[:, None, :, None], (first, tile_size, last, tile_size)
    )
    return spread.reshape(first * tile_size, last * tile_size)


def on_any_device(left_blocks, batch_blocks, left_mask, batch_mask, prune_mask):
    tile_size = left_blocks.shape[0] // left_mask.shape[0]
    left = left_blocks[:, 0, :] * widen(left_mask[:, 0, :], tile_size, jnp.bfloat16)
    right = batch_blocks[0] * widen(batch_mask[0], tile_size, jnp.bfloat16)
    product = jnp.dot(
        lax.all_gather(left, "col", axis=1, tiled=True),
        lax.all_gather(right, "row", axis=0, tiled=True),
        preferred_element_type=jnp.float32,
    )
    own_share = lax.psum_scatter(product, "layer", scatter_dimension=1, tiled=True)
    inflated = own_share * own_share * widen(prune_mask, tile_size, jnp.float32)
    col_sums = lax.psum(jnp.sum(inflated, axis=0), "row")
    total_rows = left.shape[0] * lax.axis_size("row")
    return inflated * (total_rows / (col_sums + epsilon))


def solution(mesh):
    placed = (
        P("row", "layer", "col"),
        P("layer", "row", "col"),
        P("row", "layer", "col"),
        P("layer", "row", "col"),
        P("row", ("col", "layer")),
    )
    small = mesh.shape["row"] == 4 and mesh.shape["col"] == 4 and mesh.shape["layer"] == 2
    return jax.shard_map(
        on_device if small else on_any_device,
        mesh=mesh,
        in_specs=placed,
        out_specs=P("row", ("col", "layer")),
        check_vma=False,
    )
```

```python
import functools

import jax
import jax.numpy as jnp
from jax import lax
from jax.experimental import pallas as pl
from jax.experimental.pallas import tpu as pltpu
from jax.sharding import PartitionSpec as P

epsilon = 1e-06
VMEM = pl.BlockSpec(memory_space=pltpu.VMEM)
room = pltpu.CompilerParams(vmem_limit_bytes=4 << 20)


def entry(mask, i, j):
    return mask[i : i + 1, j : j + 1] != 0


def keep_tiles(mask, turned, block, out):
    tall, wide = mask.shape[::-1] if turned else mask.shape
    high, broad = block.shape[0] // tall, block.shape[1] // wide
    for i in range(tall):
        for j in range(wide):
            at = (slice(i * high, (i + 1) * high), slice(j * broad, (j + 1) * broad))
            values = block[at]
            one = entry(mask, j, i) if turned else entry(mask, i, j)
            kept = jnp.broadcast_to(one, values.shape)
            out[at] = jnp.where(kept, values, jnp.zeros_like(values))


def tiles_kernel(*refs):
    operands, (right, left, prune), held, arrived = refs[:5], refs[5:8], refs[8:12], refs[12]
    copies = []
    for n, target in enumerate(held + (prune,)):
        parts = 4 if n in (1, 3) else 1
        tall = operands[n].shape[0] // parts
        for part in range(parts):
            at = pl.ds(part * tall, tall)
            copy = pltpu.make_async_copy(
                operands[n].at[at], target.at[at], arrived.at[len(copies)]
            )
            copy.start()
            copies.append(copy)
    for copy in copies[:5]:
        copy.wait()
    keep_tiles(held[0], False, held[1], right)
    for copy in copies[5:]:
        copy.wait()
    keep_tiles(held[2], True, held[3], left)


def tiles(*operands):
    held = [pltpu.VMEM(value.shape, value.dtype) for value in operands[:4]]
    return pl.pallas_call(
        tiles_kernel,
        out_shape=[
            jax.ShapeDtypeStruct(operands[n].shape, operands[n].dtype) for n in (1, 3, 4)
        ],
        in_specs=[pl.BlockSpec(memory_space=pltpu.HBM)] * 5,
        out_specs=[VMEM, VMEM, VMEM],
        scratch_shapes=held + [pltpu.SemaphoreType.DMA((11,))],
        compiler_params=room,
        name="tiles",
    )(*(pltpu.with_memory_space_constraint(value, pltpu.HBM) for value in operands))


def call(kernel, name, shapes, *operands, scratch=()):
    return pl.pallas_call(
        kernel,
        out_shape=shapes,
        in_specs=[VMEM] * len(operands),
        out_specs=jax.tree.map(lambda _: VMEM, shapes),
        scratch_shapes=scratch,
        compiler_params=room,
        name=name,
    )(*operands)


def swapped(value, axis, step):
    count = lax.axis_size(axis)
    return lax.ppermute(value, axis, [(i, i ^ step) for i in range(count)])


def pair_kernel(here, beside, out):
    out[0] = here[...]
    out[1] = beside[...]


def stack_kernel(*refs):
    for n, block in enumerate(refs[:-1]):
        refs[-1][n] = block[...]


def hand_kernel(block, after, out):
    out[...] = block[...]


def early_kernel(near, far, rights, after, mask, *refs):
    outs, left, held = refs[:-2], refs[-2], refs[-1]
    layer = lax.axis_index("layer")
    held[0] = near[0]
    held[1 + layer] = near[1]
    held[2 - layer] = far[0]
    held[3] = far[1]
    row, col = lax.axis_index("row"), lax.axis_index("col")
    block = lax.rem(2 * row + 1, 5)
    left[...] = held[row ^ 3 ^ col]
    (rows, depth), broad = left.shape, outs[0].shape[1]
    tall, wide = mask.shape
    share = rows // len(outs)
    lefts = [held[here ^ col] for here in (row, block, block ^ 3)]
    total = jnp.dot(
        jnp.concatenate(lefts, axis=1),
        rights[...].reshape(3 * depth, -1),
        preferred_element_type=jnp.float32,
    )
    for n, out in enumerate(outs):
        out[0:rows, :] = total[:, n * broad : (n + 1) * broad]
        out[rows : out.shape[0] - share, :] = jnp.zeros_like(
            out[rows : out.shape[0] - share, :]
        )
        for i in range(tall):
            kept = entry(mask, i, n % wide).astype(jnp.float32)
            out[rows + i : rows + i + 1, :] = jnp.broadcast_to(kept, (1, broad))
        out[out.shape[0] - share :, :] = left[n * share : (n + 1) * share, :].astype(
            jnp.float32
        )


def last_kernel(inner, outer, out):
    row = lax.axis_index("row")

    @pl.when(jnp.logical_or(row == 1, row == 2))
    def _():
        out[...] = inner[...]

    @pl.when(jnp.logical_or(row == 0, row == 3))
    def _():
        out[...] = outer[...]


def join_kernel(sizes, *refs):
    rows, half, tall, wide = sizes
    count = 2 * wide
    ours, left, theirs = refs[:count], refs[count], refs[count + 1 : -3]
    total, kept, lefts = refs[-3:]
    broad = half // wide
    share = rows // count
    depth = left.shape[1]
    layer = lax.axis_index("layer")
    crossed = jnp.logical_or(lax.axis_index("row") == 1, lax.axis_index("row") == 2)
    here = pl.multiple_of(jnp.where(crossed, depth, 0), depth)
    there = pl.multiple_of(jnp.where(crossed, 0, depth), depth)
    lefts[:, pl.ds(here, depth)] = left[...]
    for n in range(count):
        columns = slice(n * broad, (n + 1) * broad)
        total[:, columns] = ours[n][0:rows, :] + theirs[n][0:rows, :]
        entries = slice(rows, rows + kept.shape[0])
        own = layer == n // wide
        kept[:, columns] = jnp.where(own, ours[n][entries, :], theirs[n][entries, :])
        lefts[n * share : (n + 1) * share, pl.ds(there, depth)] = theirs[n][
            theirs[n].shape[0] - share :, :
        ].astype(left.dtype)


def inflate(side, sizes, joined, out, sums):
    rows, half, tall, wide = sizes
    early, kept, lefts, here, there = joined
    high = rows // tall
    columns = slice(side * half, (side + 1) * half)
    product = early[:, columns] + jnp.dot(
        lefts[...],
        jnp.concatenate([here[:, columns], there[:, columns]], axis=0),
        preferred_element_type=jnp.float32,
    )
    total = jnp.zeros((1, half), jnp.float32)
    for i in range(tall):
        at = slice(i * high, (i + 1) * high)
        keep = jnp.broadcast_to(kept[i : i + 1, columns] != 0.0, (high, half))
        value = jnp.where(keep, product[at, :] * product[at, :], 0.0)
        if out is not None:
            out[at, :] = value
        total += jnp.sum(value, axis=0, keepdims=True)
    sums[...] = total


def sums_kernel(sizes, *refs):
    for core in range(2):

        @pl.when(lax.axis_index("layer") == core)
        def _():
            inflate(1 - core, sizes, refs[:-1], None, refs[-1])


def inflate_kernel(sizes, *refs):
    for core in range(2):

        @pl.when(lax.axis_index("layer") == core)
        def _():
            inflate(core, sizes, refs[:-2], refs[-2], refs[-1])


def on_device(left_blocks, batch_blocks, left_mask, batch_mask, prune_mask):
    f32 = jnp.float32
    rows, columns = left_blocks.shape[0], batch_blocks.shape[2]
    half = columns // 2
    right, left, prune_mask = tiles(
        batch_mask[0],
        batch_blocks[0],
        jnp.transpose(left_mask, (1, 2, 0))[0],
        left_blocks[:, 0, :],
        prune_mask,
    )
    count = lax.axis_size("row")
    first = lax.ppermute(right, "row", [(0, 2), (3, 1), (1, 0), (2, 3)])
    second = lax.ppermute(right, "row", [(0, 1), (3, 2), (1, 3), (2, 0)])
    pairs = [(2, 5), (3, 4), (4, 3), (5, 2), (0, 1), (1, 0), (6, 7), (7, 6)]
    inner = lax.ppermute(right, ("row", "layer"), pairs)
    outer = lax.ppermute(first, "row", [(0, 1), (1, 0), (2, 3), (3, 2)])
    along, across = (
        [(2 * c + core, 2 * (c ^ (2 if core == turn else 1)) + core) for c in range(4) for core in (0, 1)]
        for turn in (1, 0)
    )
    beside = lax.ppermute(left, ("col", "layer"), along)
    pair = call(
        pair_kernel, "pair", jax.ShapeDtypeStruct((2,) + left.shape, left.dtype), left, beside
    )
    piece = jax.ShapeDtypeStruct((rows, half), f32)
    tall, wide = prune_mask.shape
    parts = 2 * wide
    share = rows // parts
    part = jax.ShapeDtypeStruct((rows + (tall + 7) // 8 * 8 + share, columns // parts), f32)
    block = jax.ShapeDtypeStruct(right.shape, right.dtype)
    rights = jax.ShapeDtypeStruct((3,) + right.shape, right.dtype)
    rights = call(stack_kernel, "rights", rights, right, first, second)
    handed = call(hand_kernel, "inner", block, inner, rights)
    ours = call(
        early_kernel,
        "early",
        [part] * parts + [jax.ShapeDtypeStruct(left.shape, left.dtype)],
        pair,
        lax.ppermute(pair, ("col", "layer"), across),
        rights,
        handed,
        prune_mask,
        scratch=[pltpu.VMEM((4,) + left.shape, left.dtype)],
    )
    last = call(
        last_kernel, "last", block, handed, outer
    )
    sizes = (rows, half, tall, wide)
    operands = list(call(
        functools.partial(join_kernel, sizes),
        "join",
        [
            jax.ShapeDtypeStruct((rows, columns), f32),
            jax.ShapeDtypeStruct(((tall + 7) // 8 * 8, columns), f32),
            jax.ShapeDtypeStruct((rows, 2 * left.shape[1]), left.dtype),
        ],
        *ours,
        *(swapped(value, "layer", 1) for value in ours[:-1]),
    ))
    operands += [last, swapped(last, "layer", 1)]
    line = jax.ShapeDtypeStruct((1, half), f32)
    sums = call(functools.partial(sums_kernel, sizes), "sums", line, *operands)
    inflated, sums_here = call(
        functools.partial(inflate_kernel, sizes), "inflate", [piece, line], *operands
    )
    total = sums_here
    for step in (1, 2, 3):
        pairs = [
            (2 * z + core, 2 * (z ^ step) + 1 - core)
            for z in range(count)
            for core in range(2)
        ]
        total = total + lax.ppermute(sums, ("row", "layer"), pairs)
    return inflated * (rows * count / (total + epsilon))


def widen(mask, tile_size, dtype):
    first, last = mask.shape
    spread = jnp.broadcast_to(
        mask.astype(dtype)[:, None, :, None], (first, tile_size, last, tile_size)
    )
    return spread.reshape(first * tile_size, last * tile_size)


def on_any_device(left_blocks, batch_blocks, left_mask, batch_mask, prune_mask):
    tile_size = left_blocks.shape[0] // left_mask.shape[0]
    left = left_blocks[:, 0, :] * widen(left_mask[:, 0, :], tile_size, jnp.bfloat16)
    right = batch_blocks[0] * widen(batch_mask[0], tile_size, jnp.bfloat16)
    product = jnp.dot(
        lax.all_gather(left, "col", axis=1, tiled=True),
        lax.all_gather(right, "row", axis=0, tiled=True),
        preferred_element_type=jnp.float32,
    )
    own_share = lax.psum_scatter(product, "layer", scatter_dimension=1, tiled=True)
    inflated = own_share * own_share * widen(prune_mask, tile_size, jnp.float32)
    col_sums = lax.psum(jnp.sum(inflated, axis=0), "row")
    total_rows = left.shape[0] * lax.axis_size("row")
    return inflated * (total_rows / (col_sums + epsilon))


def solution(mesh):
    placed = (
        P("row", "layer", "col"),
        P("layer", "row", "col"),
        P("row", "layer", "col"),
        P("layer", "row", "col"),
        P("row", ("col", "layer")),
    )
    small = mesh.shape["row"] == 4 and mesh.shape["col"] == 4 and mesh.shape["layer"] == 2
    return jax.shard_map(
        on_device if small else on_any_device,
        mesh=mesh,
        in_specs=placed,
        out_specs=P("row", ("col", "layer")),
        check_vma=False,
    )
```

```python
import functools

import jax
import jax.numpy as jnp
from jax import lax
from jax.experimental import pallas as pl
from jax.experimental.pallas import tpu as pltpu
from jax.sharding import PartitionSpec as P

epsilon = 1e-06
VMEM = pl.BlockSpec(memory_space=pltpu.VMEM)
room = pltpu.CompilerParams(vmem_limit_bytes=4 << 20)


def entry(mask, i, j):
    return mask[i : i + 1, j : j + 1] != 0


def keep_tiles(mask, turned, block, out):
    tall, wide = mask.shape[::-1] if turned else mask.shape
    high, broad = block.shape[0] // tall, block.shape[1] // wide
    for i in range(tall):
        for j in range(wide):
            at = (slice(i * high, (i + 1) * high), slice(j * broad, (j + 1) * broad))
            values = block[at]
            one = entry(mask, j, i) if turned else entry(mask, i, j)
            kept = jnp.broadcast_to(one, values.shape)
            out[at] = jnp.where(kept, values, jnp.zeros_like(values))


def tiles_kernel(*refs):
    operands, (right, left, prune), held, arrived = refs[:5], refs[5:8], refs[8:12], refs[12]
    copies = []
    for n, target in enumerate(held + (prune,)):
        parts = 4 if n in (1, 3) else 1
        tall = operands[n].shape[0] // parts
        for part in range(parts):
            at = pl.ds(part * tall, tall)
            copy = pltpu.make_async_copy(
                operands[n].at[at], target.at[at], arrived.at[len(copies)]
            )
            copy.start()
            copies.append(copy)
    for copy in copies[:5]:
        copy.wait()
    keep_tiles(held[0], False, held[1], right)
    for copy in copies[5:]:
        copy.wait()
    keep_tiles(held[2], True, held[3], left)


def tiles(*operands):
    held = [pltpu.VMEM(value.shape, value.dtype) for value in operands[:4]]
    return pl.pallas_call(
        tiles_kernel,
        out_shape=[
            jax.ShapeDtypeStruct(operands[n].shape, operands[n].dtype) for n in (1, 3, 4)
        ],
        in_specs=[pl.BlockSpec(memory_space=pltpu.HBM)] * 5,
        out_specs=[VMEM, VMEM, VMEM],
        scratch_shapes=held + [pltpu.SemaphoreType.DMA((11,))],
        compiler_params=room,
        name="tiles",
    )(*(pltpu.with_memory_space_constraint(value, pltpu.HBM) for value in operands))


def call(kernel, name, shapes, *operands, scratch=()):
    return pl.pallas_call(
        kernel,
        out_shape=shapes,
        in_specs=[VMEM] * len(operands),
        out_specs=jax.tree.map(lambda _: VMEM, shapes),
        scratch_shapes=scratch,
        compiler_params=room,
        name=name,
    )(*operands)


def swapped(value, axis, step):
    count = lax.axis_size(axis)
    return lax.ppermute(value, axis, [(i, i ^ step) for i in range(count)])


def pair_kernel(here, beside, out):
    out[0] = here[...]
    out[1] = beside[...]


def stack_kernel(*refs):
    for n, block in enumerate(refs[:-1]):
        refs[-1][n] = block[...]


def hand_kernel(block, after, out):
    out[...] = block[...]


def early_kernel(near, far, rights, after, mask, *refs):
    outs, left, held = refs[:-2], refs[-2], refs[-1]
    layer = lax.axis_index("layer")
    held[0] = near[0]
    held[1 + layer] = near[1]
    held[2 - layer] = far[0]
    held[3] = far[1]
    row, col = lax.axis_index("row"), lax.axis_index("col")
    block = lax.rem(2 * row + 1, 5)
    left[...] = held[row ^ 3 ^ col]
    (rows, depth), broad = left.shape, outs[0].shape[1]
    tall, wide = mask.shape
    share = rows // len(outs)
    lefts = [held[here ^ col] for here in (row, block, block ^ 3)]
    total = jnp.dot(
        jnp.concatenate(lefts, axis=1),
        rights[...].reshape(3 * depth, -1),
        preferred_element_type=jnp.float32,
    )
    for n, out in enumerate(outs):
        out[0:rows, :] = total[:, n * broad : (n + 1) * broad]
        out[rows : out.shape[0] - share, :] = jnp.zeros_like(
            out[rows : out.shape[0] - share, :]
        )
        for i in range(tall):
            kept = entry(mask, i, n % wide).astype(jnp.float32)
            out[rows + i : rows + i + 1, :] = jnp.broadcast_to(kept, (1, broad))
        out[out.shape[0] - share :, :] = left[n * share : (n + 1) * share, :].astype(
            jnp.float32
        )


def last_kernel(inner, outer, out):
    row = lax.axis_index("row")

    @pl.when(jnp.logical_or(row == 1, row == 2))
    def _():
        out[...] = inner[...]

    @pl.when(jnp.logical_or(row == 0, row == 3))
    def _():
        out[...] = outer[...]


def join_kernel(sizes, *refs):
    rows, half, tall, wide = sizes
    count = 2 * wide
    ours, left, theirs, last = refs[:count], refs[count], refs[count + 1 : -5], refs[-5]
    total, kept, lefts, other = refs[-4:]
    broad = half // wide
    share = rows // count
    depth = left.shape[1]
    layer = lax.axis_index("layer")
    crossed = jnp.logical_or(lax.axis_index("row") == 1, lax.axis_index("row") == 2)
    for n in range(count):
        columns = slice(n * broad, (n + 1) * broad)
        total[:, columns] = ours[n][0:rows, :] + theirs[n][0:rows, :]
        entries = slice(rows, rows + kept.shape[0])
        own = layer == n // wide
        kept[:, columns] = jnp.where(own, ours[n][entries, :], theirs[n][entries, :])
        other[n * share : (n + 1) * share, :] = theirs[n][
            theirs[n].shape[0] - share :, :
        ].astype(left.dtype)
    mine = jnp.where(crossed, other[...], left[...])
    lefts[...] = jnp.where(crossed, left[...], other[...])
    total[...] += jnp.dot(mine, last[...], preferred_element_type=jnp.float32)


def inflate(side, sizes, joined, out, sums):
    rows, half, tall, wide = sizes
    early, kept, lefts, there = joined
    high = rows // tall
    columns = slice(side * half, (side + 1) * half)
    product = early[:, columns] + jnp.dot(
        lefts[...],
        there[:, columns],
        preferred_element_type=jnp.float32,
    )
    total = jnp.zeros((1, half), jnp.float32)
    for i in range(tall):
        at = slice(i * high, (i + 1) * high)
        keep = jnp.broadcast_to(kept[i : i + 1, columns] != 0.0, (high, half))
        value = jnp.where(keep, product[at, :] * product[at, :], 0.0)
        if out is not None:
            out[at, :] = value
        total += jnp.sum(value, axis=0, keepdims=True)
    sums[...] = total


def sums_kernel(sizes, *refs):
    for core in range(2):

        @pl.when(lax.axis_index("layer") == core)
        def _():
            inflate(1 - core, sizes, refs[:-1], None, refs[-1])


def inflate_kernel(sizes, *refs):
    for core in range(2):

        @pl.when(lax.axis_index("layer") == core)
        def _():
            inflate(core, sizes, refs[:-2], refs[-2], refs[-1])


def on_device(left_blocks, batch_blocks, left_mask, batch_mask, prune_mask):
    f32 = jnp.float32
    rows, columns = left_blocks.shape[0], batch_blocks.shape[2]
    half = columns // 2
    right, left, prune_mask = tiles(
        batch_mask[0],
        batch_blocks[0],
        jnp.transpose(left_mask, (1, 2, 0))[0],
        left_blocks[:, 0, :],
        prune_mask,
    )
    count = lax.axis_size("row")
    first = lax.ppermute(right, "row", [(0, 2), (3, 1), (1, 0), (2, 3)])
    second = lax.ppermute(right, "row", [(0, 1), (3, 2), (1, 3), (2, 0)])
    pairs = [(2, 5), (3, 4), (4, 3), (5, 2), (0, 1), (1, 0), (6, 7), (7, 6)]
    inner = lax.ppermute(right, ("row", "layer"), pairs)
    outer = lax.ppermute(first, "row", [(0, 1), (1, 0), (2, 3), (3, 2)])
    along, across = (
        [(2 * c + core, 2 * (c ^ (2 if core == turn else 1)) + core) for c in range(4) for core in (0, 1)]
        for turn in (1, 0)
    )
    beside = lax.ppermute(left, ("col", "layer"), along)
    pair = call(
        pair_kernel, "pair", jax.ShapeDtypeStruct((2,) + left.shape, left.dtype), left, beside
    )
    piece = jax.ShapeDtypeStruct((rows, half), f32)
    tall, wide = prune_mask.shape
    parts = 2 * wide
    share = rows // parts
    part = jax.ShapeDtypeStruct((rows + (tall + 7) // 8 * 8 + share, columns // parts), f32)
    block = jax.ShapeDtypeStruct(right.shape, right.dtype)
    rights = jax.ShapeDtypeStruct((3,) + right.shape, right.dtype)
    rights = call(stack_kernel, "rights", rights, right, first, second)
    handed = call(hand_kernel, "inner", block, inner, rights)
    ours = call(
        early_kernel,
        "early",
        [part] * parts + [jax.ShapeDtypeStruct(left.shape, left.dtype)],
        pair,
        lax.ppermute(pair, ("col", "layer"), across),
        rights,
        handed,
        prune_mask,
        scratch=[pltpu.VMEM((4,) + left.shape, left.dtype)],
    )
    last = call(
        last_kernel, "last", block, handed, outer
    )
    sizes = (rows, half, tall, wide)
    operands = list(call(
        functools.partial(join_kernel, sizes),
        "join",
        [
            jax.ShapeDtypeStruct((rows, columns), f32),
            jax.ShapeDtypeStruct(((tall + 7) // 8 * 8, columns), f32),
            jax.ShapeDtypeStruct(left.shape, left.dtype),
        ],
        *ours,
        *(swapped(value, "layer", 1) for value in ours[:-1]),
        last,
        scratch=[pltpu.VMEM(left.shape, left.dtype)],
    ))
    operands.append(swapped(last, "layer", 1))
    line = jax.ShapeDtypeStruct((1, half), f32)
    sums = call(functools.partial(sums_kernel, sizes), "sums", line, *operands)
    inflated, sums_here = call(
        functools.partial(inflate_kernel, sizes), "inflate", [piece, line], *operands
    )
    total = sums_here
    for step in (3, 2, 1):
        pairs = [
            (2 * z + core, 2 * (z ^ step) + 1 - core)
            for z in range(count)
            for core in range(2)
        ]
        total = total + lax.ppermute(sums, ("row", "layer"), pairs)
    return inflated * (rows * count / (total + epsilon))


def widen(mask, tile_size, dtype):
    first, last = mask.shape
    spread = jnp.broadcast_to(
        mask.astype(dtype)[:, None, :, None], (first, tile_size, last, tile_size)
    )
    return spread.reshape(first * tile_size, last * tile_size)


def on_any_device(left_blocks, batch_blocks, left_mask, batch_mask, prune_mask):
    tile_size = left_blocks.shape[0] // left_mask.shape[0]
    left = left_blocks[:, 0, :] * widen(left_mask[:, 0, :], tile_size, jnp.bfloat16)
    right = batch_blocks[0] * widen(batch_mask[0], tile_size, jnp.bfloat16)
    product = jnp.dot(
        lax.all_gather(left, "col", axis=1, tiled=True),
        lax.all_gather(right, "row", axis=0, tiled=True),
        preferred_element_type=jnp.float32,
    )
    own_share = lax.psum_scatter(product, "layer", scatter_dimension=1, tiled=True)
    inflated = own_share * own_share * widen(prune_mask, tile_size, jnp.float32)
    col_sums = lax.psum(jnp.sum(inflated, axis=0), "row")
    total_rows = left.shape[0] * lax.axis_size("row")
    return inflated * (total_rows / (col_sums + epsilon))


def solution(mesh):
    placed = (
        P("row", "layer", "col"),
        P("layer", "row", "col"),
        P("row", "layer", "col"),
        P("layer", "row", "col"),
        P("row", ("col", "layer")),
    )
    small = mesh.shape["row"] == 4 and mesh.shape["col"] == 4 and mesh.shape["layer"] == 2
    return jax.shard_map(
        on_device if small else on_any_device,
        mesh=mesh,
        in_specs=placed,
        out_specs=P("row", ("col", "layer")),
        check_vma=False,
    )
```

```python
import functools

import jax
import jax.numpy as jnp
from jax import lax
from jax.experimental import pallas as pl
from jax.experimental.pallas import tpu as pltpu
from jax.sharding import PartitionSpec as P

epsilon = 1e-06
VMEM = pl.BlockSpec(memory_space=pltpu.VMEM)
room = pltpu.CompilerParams(vmem_limit_bytes=4 << 20)


def entry(mask, i, j):
    return mask[i : i + 1, j : j + 1] != 0


def keep_tiles(mask, turned, block, out):
    tall, wide = mask.shape[::-1] if turned else mask.shape
    high, broad = block.shape[0] // tall, block.shape[1] // wide
    for i in range(tall):
        for j in range(wide):
            at = (slice(i * high, (i + 1) * high), slice(j * broad, (j + 1) * broad))
            values = block[at]
            one = entry(mask, j, i) if turned else entry(mask, i, j)
            kept = jnp.broadcast_to(one, values.shape)
            out[at] = jnp.where(kept, values, jnp.zeros_like(values))


def tiles_kernel(*refs):
    operands, (right, left, prune), held, arrived = refs[:5], refs[5:8], refs[8:12], refs[12]
    copies = []
    for n, target in enumerate(held + (prune,)):
        parts = {1: 2, 3: 2}.get(n, 1)
        tall = operands[n].shape[0] // parts
        for part in range(parts):
            at = pl.ds(part * tall, tall)
            copy = pltpu.make_async_copy(
                operands[n].at[at], target.at[at], arrived.at[len(copies)]
            )
            copy.start()
            copies.append(copy)
    for copy in copies[:3]:
        copy.wait()
    keep_tiles(held[0], False, held[1], right)
    for copy in copies[3:]:
        copy.wait()
    keep_tiles(held[2], True, held[3], left)


def tiles(*operands):
    held = [pltpu.VMEM(value.shape, value.dtype) for value in operands[:4]]
    return pl.pallas_call(
        tiles_kernel,
        out_shape=[
            jax.ShapeDtypeStruct(operands[n].shape, operands[n].dtype) for n in (1, 3, 4)
        ],
        in_specs=[pl.BlockSpec(memory_space=pltpu.HBM)] * 5,
        out_specs=[VMEM, VMEM, VMEM],
        scratch_shapes=held + [pltpu.SemaphoreType.DMA((7,))],
        compiler_params=room,
        name="tiles",
    )(*(pltpu.with_memory_space_constraint(value, pltpu.HBM) for value in operands))


def call(kernel, name, shapes, *operands, scratch=()):
    return pl.pallas_call(
        kernel,
        out_shape=shapes,
        in_specs=[VMEM] * len(operands),
        out_specs=jax.tree.map(lambda _: VMEM, shapes),
        scratch_shapes=scratch,
        compiler_params=room,
        name=name,
    )(*operands)


def swapped(value, axis, step):
    count = lax.axis_size(axis)
    return lax.ppermute(value, axis, [(i, i ^ step) for i in range(count)])


def pair_kernel(here, beside, out):
    out[0] = here[...]
    out[1] = beside[...]


def stack_kernel(*refs):
    for n, block in enumerate(refs[:-1]):
        refs[-1][n] = block[...]


def hand_kernel(block, after, out):
    out[...] = block[...]


def early_kernel(near, far, rights, after, mask, *refs):
    outs, left, held = refs[:-2], refs[-2], refs[-1]
    layer = lax.axis_index("layer")
    held[0] = near[0]
    held[1 + layer] = near[1]
    held[2 - layer] = far[0]
    held[3] = far[1]
    row, col = lax.axis_index("row"), lax.axis_index("col")
    block = lax.rem(2 * row + 1, 5)
    left[...] = held[row ^ 3 ^ col]
    (rows, depth), broad = left.shape, outs[0].shape[1]
    tall, wide = mask.shape
    share = rows // len(outs)
    lefts = [held[here ^ col] for here in (row, block, block ^ 3)]
    total = jnp.dot(
        jnp.concatenate(lefts, axis=1),
        rights[...].reshape(3 * depth, -1),
        preferred_element_type=jnp.float32,
    )
    for n, out in enumerate(outs):
        out[0:rows, :] = total[:, n * broad : (n + 1) * broad]
        out[rows : out.shape[0] - share, :] = jnp.zeros_like(
            out[rows : out.shape[0] - share, :]
        )
        for i in range(tall):
            kept = entry(mask, i, n % wide).astype(jnp.float32)
            out[rows + i : rows + i + 1, :] = jnp.broadcast_to(kept, (1, broad))
        out[out.shape[0] - share :, :] = left[n * share : (n + 1) * share, :].astype(
            jnp.float32
        )


def last_kernel(inner, outer, out):
    row = lax.axis_index("row")

    @pl.when(jnp.logical_or(row == 1, row == 2))
    def _():
        out[...] = inner[...]

    @pl.when(jnp.logical_or(row == 0, row == 3))
    def _():
        out[...] = outer[...]


def join_kernel(sizes, *refs):
    rows, half, tall, wide = sizes
    count = 2 * wide
    ours, left, theirs = refs[:count], refs[count], refs[count + 1 : -3]
    total, kept, lefts = refs[-3:]
    broad = half // wide
    share = rows // count
    depth = left.shape[1]
    layer = lax.axis_index("layer")
    crossed = jnp.logical_or(lax.axis_index("row") == 1, lax.axis_index("row") == 2)
    here = pl.multiple_of(jnp.where(crossed, depth, 0), depth)
    there = pl.multiple_of(jnp.where(crossed, 0, depth), depth)
    lefts[:, pl.ds(here, depth)] = left[...]
    for n in range(count):
        columns = slice(n * broad, (n + 1) * broad)
        total[:, columns] = ours[n][0:rows, :] + theirs[n][0:rows, :]
        entries = slice(rows, rows + kept.shape[0])
        own = layer == n // wide
        kept[:, columns] = jnp.where(own, ours[n][entries, :], theirs[n][entries, :])
        lefts[n * share : (n + 1) * share, pl.ds(there, depth)] = theirs[n][
            theirs[n].shape[0] - share :, :
        ].astype(left.dtype)


def inflate(side, sizes, joined, out, sums):
    rows, half, tall, wide = sizes
    early, kept, lefts, here, there = joined
    high = rows // tall
    columns = slice(side * half, (side + 1) * half)
    product = early[:, columns] + jnp.dot(
        lefts[...],
        jnp.concatenate([here[:, columns], there[:, columns]], axis=0),
        preferred_element_type=jnp.float32,
    )
    total = jnp.zeros((1, half), jnp.float32)
    for i in range(tall):
        at = slice(i * high, (i + 1) * high)
        keep = jnp.broadcast_to(kept[i : i + 1, columns] != 0.0, (high, half))
        value = jnp.where(keep, product[at, :] * product[at, :], 0.0)
        if out is not None:
            out[at, :] = value
        total += jnp.sum(value, axis=0, keepdims=True)
    sums[...] = total


def sums_kernel(sizes, *refs):
    for core in range(2):

        @pl.when(lax.axis_index("layer") == core)
        def _():
            inflate(1 - core, sizes, refs[:-1], None, refs[-1])


def inflate_kernel(sizes, *refs):
    for core in range(2):

        @pl.when(lax.axis_index("layer") == core)
        def _():
            inflate(core, sizes, refs[:-2], refs[-2], refs[-1])


def on_device(left_blocks, batch_blocks, left_mask, batch_mask, prune_mask):
    f32 = jnp.float32
    rows, columns = left_blocks.shape[0], batch_blocks.shape[2]
    half = columns // 2
    right, left, prune_mask = tiles(
        batch_mask[0],
        batch_blocks[0],
        jnp.transpose(left_mask, (1, 2, 0))[0],
        left_blocks[:, 0, :],
        prune_mask,
    )
    count = lax.axis_size("row")
    first = lax.ppermute(right, "row", [(0, 2), (3, 1), (1, 0), (2, 3)])
    second = lax.ppermute(right, "row", [(0, 1), (3, 2), (1, 3), (2, 0)])
    pairs = [(2, 5), (3, 4), (4, 3), (5, 2), (0, 1), (1, 0), (6, 7), (7, 6)]
    inner = lax.ppermute(right, ("row", "layer"), pairs)
    outer = lax.ppermute(first, "row", [(0, 1), (1, 0), (2, 3), (3, 2)])
    along, across = (
        [(2 * c + core, 2 * (c ^ (2 if core == turn else 1)) + core) for c in range(4) for core in (0, 1)]
        for turn in (1, 0)
    )
    beside = lax.ppermute(left, ("col", "layer"), along)
    pair = call(
        pair_kernel, "pair", jax.ShapeDtypeStruct((2,) + left.shape, left.dtype), left, beside
    )
    piece = jax.ShapeDtypeStruct((rows, half), f32)
    tall, wide = prune_mask.shape
    parts = 2 * wide
    share = rows // parts
    part = jax.ShapeDtypeStruct((rows + (tall + 7) // 8 * 8 + share, columns // parts), f32)
    block = jax.ShapeDtypeStruct(right.shape, right.dtype)
    rights = jax.ShapeDtypeStruct((3,) + right.shape, right.dtype)
    rights = call(stack_kernel, "rights", rights, right, first, second)
    handed = call(hand_kernel, "inner", block, inner, rights)
    ours = call(
        early_kernel,
        "early",
        [part] * parts + [jax.ShapeDtypeStruct(left.shape, left.dtype)],
        pair,
        lax.ppermute(pair, ("col", "layer"), across),
        rights,
        handed,
        prune_mask,
        scratch=[pltpu.VMEM((4,) + left.shape, left.dtype)],
    )
    last = call(
        last_kernel, "last", block, handed, outer
    )
    sizes = (rows, half, tall, wide)
    operands = list(call(
        functools.partial(join_kernel, sizes),
        "join",
        [
            jax.ShapeDtypeStruct((rows, columns), f32),
            jax.ShapeDtypeStruct(((tall + 7) // 8 * 8, columns), f32),
            jax.ShapeDtypeStruct((rows, 2 * left.shape[1]), left.dtype),
        ],
        *ours,
        *(swapped(value, "layer", 1) for value in ours[:-1]),
    ))
    operands += [last, swapped(last, "layer", 1)]
    line = jax.ShapeDtypeStruct((1, half), f32)
    sums = call(functools.partial(sums_kernel, sizes), "sums", line, *operands)
    inflated, sums_here = call(
        functools.partial(inflate_kernel, sizes), "inflate", [piece, line], *operands
    )
    total = sums_here
    for step in (1, 2, 3):
        pairs = [
            (2 * z + core, 2 * (z ^ step) + 1 - core)
            for z in range(count)
            for core in range(2)
        ]
        total = total + lax.ppermute(sums, ("row", "layer"), pairs)
    return inflated * (rows * count / (total + epsilon))


def widen(mask, tile_size, dtype):
    first, last = mask.shape
    spread = jnp.broadcast_to(
        mask.astype(dtype)[:, None, :, None], (first, tile_size, last, tile_size)
    )
    return spread.reshape(first * tile_size, last * tile_size)


def on_any_device(left_blocks, batch_blocks, left_mask, batch_mask, prune_mask):
    tile_size = left_blocks.shape[0] // left_mask.shape[0]
    left = left_blocks[:, 0, :] * widen(left_mask[:, 0, :], tile_size, jnp.bfloat16)
    right = batch_blocks[0] * widen(batch_mask[0], tile_size, jnp.bfloat16)
    product = jnp.dot(
        lax.all_gather(left, "col", axis=1, tiled=True),
        lax.all_gather(right, "row", axis=0, tiled=True),
        preferred_element_type=jnp.float32,
    )
    own_share = lax.psum_scatter(product, "layer", scatter_dimension=1, tiled=True)
    inflated = own_share * own_share * widen(prune_mask, tile_size, jnp.float32)
    col_sums = lax.psum(jnp.sum(inflated, axis=0), "row")
    total_rows = left.shape[0] * lax.axis_size("row")
    return inflated * (total_rows / (col_sums + epsilon))


def solution(mesh):
    placed = (
        P("row", "layer", "col"),
        P("layer", "row", "col"),
        P("row", "layer", "col"),
        P("layer", "row", "col"),
        P("row", ("col", "layer")),
    )
    small = mesh.shape["row"] == 4 and mesh.shape["col"] == 4 and mesh.shape["layer"] == 2
    return jax.shard_map(
        on_device if small else on_any_device,
        mesh=mesh,
        in_specs=placed,
        out_specs=P("row", ("col", "layer")),
        check_vma=False,
    )
```

```python
import functools

import jax
import jax.numpy as jnp
from jax import lax
from jax.experimental import pallas as pl
from jax.experimental.pallas import tpu as pltpu
from jax.sharding import PartitionSpec as P

epsilon = 1e-06
VMEM = pl.BlockSpec(memory_space=pltpu.VMEM)
room = pltpu.CompilerParams(vmem_limit_bytes=4 << 20)


def entry(mask, i, j):
    return mask[i : i + 1, j : j + 1] != 0


def keep_tiles(mask, turned, block, out):
    tall, wide = mask.shape[::-1] if turned else mask.shape
    high, broad = block.shape[0] // tall, block.shape[1] // wide
    for i in range(tall):
        for j in range(wide):
            at = (slice(i * high, (i + 1) * high), slice(j * broad, (j + 1) * broad))
            values = block[at]
            one = entry(mask, j, i) if turned else entry(mask, i, j)
            kept = jnp.broadcast_to(one, values.shape)
            out[at] = jnp.where(kept, values, jnp.zeros_like(values))


def tiles_kernel(*refs):
    operands, (right, left, prune), held, arrived = refs[:5], refs[5:8], refs[8:12], refs[12]
    copies = []
    for n, target in enumerate(held + (prune,)):
        parts = 4 if n in (1, 3) else 1
        tall = operands[n].shape[0] // parts
        for part in range(parts):
            at = pl.ds(part * tall, tall)
            copy = pltpu.make_async_copy(
                operands[n].at[at], target.at[at], arrived.at[len(copies)]
            )
            copy.start()
            copies.append(copy)
    for copy in copies[:5]:
        copy.wait()
    keep_tiles(held[0], False, held[1], right)
    for copy in copies[5:]:
        copy.wait()
    keep_tiles(held[2], True, held[3], left)


def tiles(*operands):
    held = [pltpu.VMEM(value.shape, value.dtype) for value in operands[:4]]
    return pl.pallas_call(
        tiles_kernel,
        out_shape=[
            jax.ShapeDtypeStruct(operands[n].shape, operands[n].dtype) for n in (1, 3, 4)
        ],
        in_specs=[pl.BlockSpec(memory_space=pltpu.HBM)] * 5,
        out_specs=[VMEM, VMEM, VMEM],
        scratch_shapes=held + [pltpu.SemaphoreType.DMA((11,))],
        compiler_params=room,
        name="tiles",
    )(*(pltpu.with_memory_space_constraint(value, pltpu.HBM) for value in operands))


def call(kernel, name, shapes, *operands, scratch=()):
    return pl.pallas_call(
        kernel,
        out_shape=shapes,
        in_specs=[VMEM] * len(operands),
        out_specs=jax.tree.map(lambda _: VMEM, shapes),
        scratch_shapes=scratch,
        compiler_params=room,
        name=name,
    )(*operands)


def swapped(value, axis, step):
    count = lax.axis_size(axis)
    return lax.ppermute(value, axis, [(i, i ^ step) for i in range(count)])


def pair_kernel(here, beside, out):
    out[0] = here[...]
    out[1] = beside[...]


def stack_kernel(*refs):
    for n, block in enumerate(refs[:-1]):
        refs[-1][n] = block[...]


def hand_kernel(block, after, out):
    out[...] = block[...]


def early_kernel(near, far, rights, after, mask, *refs):
    outs, left, held = refs[:-2], refs[-2], refs[-1]
    layer = lax.axis_index("layer")
    held[0] = near[0]
    held[1 + layer] = near[1]
    held[2 - layer] = far[0]
    held[3] = far[1]
    row, col = lax.axis_index("row"), lax.axis_index("col")
    block = lax.rem(2 * row + 1, 5)
    left[...] = held[row ^ 3 ^ col]
    (rows, depth), broad = left.shape, outs[0].shape[1]
    tall, wide = mask.shape
    share = rows // len(outs)
    lefts = [held[here ^ col] for here in (row, block, block ^ 3)]
    total = jnp.dot(
        jnp.concatenate(lefts, axis=1),
        rights[...].reshape(3 * depth, -1),
        preferred_element_type=jnp.float32,
    )
    for n, out in enumerate(outs):
        out[0:rows, :] = total[:, n * broad : (n + 1) * broad]
        out[rows : out.shape[0] - share, :] = jnp.zeros_like(
            out[rows : out.shape[0] - share, :]
        )
        for i in range(tall):
            kept = entry(mask, i, n % wide).astype(jnp.float32)
            out[rows + i : rows + i + 1, :] = jnp.broadcast_to(kept, (1, broad))
        out[out.shape[0] - share :, :] = left[n * share : (n + 1) * share, :].astype(
            jnp.float32
        )


def last_kernel(inner, outer, out):
    row = lax.axis_index("row")

    @pl.when(jnp.logical_or(row == 1, row == 2))
    def _():
        out[...] = inner[...]

    @pl.when(jnp.logical_or(row == 0, row == 3))
    def _():
        out[...] = outer[...]


def join_kernel(sizes, *refs):
    rows, half, tall, wide = sizes
    count = 2 * wide
    ours, left, theirs = refs[:count], refs[count], refs[count + 1 : -3]
    total, kept, lefts = refs[-3:]
    broad = half // wide
    share = rows // count
    depth = left.shape[1]
    layer = lax.axis_index("layer")
    crossed = jnp.logical_or(lax.axis_index("row") == 1, lax.axis_index("row") == 2)
    here = pl.multiple_of(jnp.where(crossed, depth, 0), depth)
    there = pl.multiple_of(jnp.where(crossed, 0, depth), depth)
    lefts[:, pl.ds(here, depth)] = left[...]
    for n in range(count):
        columns = slice(n * broad, (n + 1) * broad)
        total[:, columns] = ours[n][0:rows, :] + theirs[n][0:rows, :]
        entries = slice(rows, rows + kept.shape[0])
        own = layer == n // wide
        kept[:, columns] = jnp.where(own, ours[n][entries, :], theirs[n][entries, :])
        lefts[n * share : (n + 1) * share, pl.ds(there, depth)] = theirs[n][
            theirs[n].shape[0] - share :, :
        ].astype(left.dtype)


def inflate(side, sizes, joined, out, sums):
    rows, half, tall, wide = sizes
    early, kept, lefts, here, there = joined
    high = rows // tall
    columns = slice(side * half, (side + 1) * half)
    product = early[:, columns] + jnp.dot(
        lefts[...],
        jnp.concatenate([here[:, columns], there[:, columns]], axis=0),
        preferred_element_type=jnp.float32,
    )
    total = jnp.zeros((1, half), jnp.float32)
    for i in range(tall):
        at = slice(i * high, (i + 1) * high)
        keep = jnp.broadcast_to(kept[i : i + 1, columns] != 0.0, (high, half))
        value = jnp.where(keep, product[at, :] * product[at, :], 0.0)
        if out is not None:
            out[at, :] = value
        total += jnp.sum(value, axis=0, keepdims=True)
    sums[...] = total


def sums_kernel(sizes, *refs):
    for core in range(2):

        @pl.when(lax.axis_index("layer") == core)
        def _():
            inflate(1 - core, sizes, refs[:-1], None, refs[-1])


def inflate_kernel(sizes, *refs):
    for core in range(2):

        @pl.when(lax.axis_index("layer") == core)
        def _():
            inflate(core, sizes, refs[:-2], refs[-2], refs[-1])


def on_device(left_blocks, batch_blocks, left_mask, batch_mask, prune_mask):
    f32 = jnp.float32
    rows, columns = left_blocks.shape[0], batch_blocks.shape[2]
    half = columns // 2
    right, left, prune_mask = tiles(
        batch_mask[0],
        batch_blocks[0],
        jnp.transpose(left_mask, (1, 2, 0))[0],
        left_blocks[:, 0, :],
        prune_mask,
    )
    count = lax.axis_size("row")
    first = lax.ppermute(right, "row", [(0, 2), (3, 1), (1, 0), (2, 3)])
    second = lax.ppermute(right, "row", [(0, 1), (3, 2), (1, 3), (2, 0)])
    pairs = [(2, 5), (3, 4), (4, 3), (5, 2), (0, 1), (1, 0), (6, 7), (7, 6)]
    inner = lax.ppermute(right, ("row", "layer"), pairs)
    pairs = [(2 * s + l, 2 * t + l) for s, t in ((1, 0), (2, 3)) for l in (0, 1)]
    pairs += [(2 * s + l, 2 * t + 1 - l) for s, t in ((0, 1), (3, 2)) for l in (0, 1)]
    outer = lax.ppermute(first, ("row", "layer"), pairs)
    along, across = (
        [(2 * c + core, 2 * (c ^ (2 if core == turn else 1)) + core) for c in range(4) for core in (0, 1)]
        for turn in (1, 0)
    )
    beside = lax.ppermute(left, ("col", "layer"), along)
    pair = call(
        pair_kernel, "pair", jax.ShapeDtypeStruct((2,) + left.shape, left.dtype), left, beside
    )
    piece = jax.ShapeDtypeStruct((rows, half), f32)
    tall, wide = prune_mask.shape
    parts = 2 * wide
    share = rows // parts
    part = jax.ShapeDtypeStruct((rows + (tall + 7) // 8 * 8 + share, columns // parts), f32)
    block = jax.ShapeDtypeStruct(right.shape, right.dtype)
    rights = jax.ShapeDtypeStruct((3,) + right.shape, right.dtype)
    rights = call(stack_kernel, "rights", rights, right, first, second)
    handed = call(hand_kernel, "inner", block, inner, rights)
    ours = call(
        early_kernel,
        "early",
        [part] * parts + [jax.ShapeDtypeStruct(left.shape, left.dtype)],
        pair,
        lax.ppermute(pair, ("col", "layer"), across),
        rights,
        handed,
        prune_mask,
        scratch=[pltpu.VMEM((4,) + left.shape, left.dtype)],
    )
    last = call(
        last_kernel, "last", block, handed, outer
    )
    sizes = (rows, half, tall, wide)
    operands = list(call(
        functools.partial(join_kernel, sizes),
        "join",
        [
            jax.ShapeDtypeStruct((rows, columns), f32),
            jax.ShapeDtypeStruct(((tall + 7) // 8 * 8, columns), f32),
            jax.ShapeDtypeStruct((rows, 2 * left.shape[1]), left.dtype),
        ],
        *ours,
        *(swapped(value, "layer", 1) for value in ours[:-1]),
    ))
    operands += [last, swapped(last, "layer", 1)]
    line = jax.ShapeDtypeStruct((1, half), f32)
    sums = call(functools.partial(sums_kernel, sizes), "sums", line, *operands)
    inflated, sums_here = call(
        functools.partial(inflate_kernel, sizes), "inflate", [piece, line], *operands
    )
    total = sums_here
    for step in (1, 2, 3):
        pairs = [
            (2 * z + core, 2 * (z ^ step) + 1 - core)
            for z in range(count)
            for core in range(2)
        ]
        total = total + lax.ppermute(sums, ("row", "layer"), pairs)
    return inflated * (rows * count / (total + epsilon))


def widen(mask, tile_size, dtype):
    first, last = mask.shape
    spread = jnp.broadcast_to(
        mask.astype(dtype)[:, None, :, None], (first, tile_size, last, tile_size)
    )
    return spread.reshape(first * tile_size, last * tile_size)


def on_any_device(left_blocks, batch_blocks, left_mask, batch_mask, prune_mask):
    tile_size = left_blocks.shape[0] // left_mask.shape[0]
    left = left_blocks[:, 0, :] * widen(left_mask[:, 0, :], tile_size, jnp.bfloat16)
    right = batch_blocks[0] * widen(batch_mask[0], tile_size, jnp.bfloat16)
    product = jnp.dot(
        lax.all_gather(left, "col", axis=1, tiled=True),
        lax.all_gather(right, "row", axis=0, tiled=True),
        preferred_element_type=jnp.float32,
    )
    own_share = lax.psum_scatter(product, "layer", scatter_dimension=1, tiled=True)
    inflated = own_share * own_share * widen(prune_mask, tile_size, jnp.float32)
    col_sums = lax.psum(jnp.sum(inflated, axis=0), "row")
    total_rows = left.shape[0] * lax.axis_size("row")
    return inflated * (total_rows / (col_sums + epsilon))


def solution(mesh):
    placed = (
        P("row", "layer", "col"),
        P("layer", "row", "col"),
        P("row", "layer", "col"),
        P("layer", "row", "col"),
        P("row", ("col", "layer")),
    )
    small = mesh.shape["row"] == 4 and mesh.shape["col"] == 4 and mesh.shape["layer"] == 2
    return jax.shard_map(
        on_device if small else on_any_device,
        mesh=mesh,
        in_specs=placed,
        out_specs=P("row", ("col", "layer")),
        check_vma=False,
    )
```

```python
import functools

import jax
import jax.numpy as jnp
from jax import lax
from jax.experimental import pallas as pl
from jax.experimental.pallas import tpu as pltpu
from jax.sharding import PartitionSpec as P

epsilon = 1e-06
VMEM = pl.BlockSpec(memory_space=pltpu.VMEM)
room = pltpu.CompilerParams(vmem_limit_bytes=4 << 20)


def entry(mask, i, j):
    return mask[i : i + 1, j : j + 1] != 0


def keep_tiles(mask, turned, block, out):
    tall, wide = mask.shape[::-1] if turned else mask.shape
    high, broad = block.shape[0] // tall, block.shape[1] // wide
    for i in range(tall):
        for j in range(wide):
            at = (slice(i * high, (i + 1) * high), slice(j * broad, (j + 1) * broad))
            values = block[at]
            one = entry(mask, j, i) if turned else entry(mask, i, j)
            kept = jnp.broadcast_to(one, values.shape)
            out[at] = jnp.where(kept, values, jnp.zeros_like(values))


def tiles_kernel(*refs):
    operands, (right, left, prune), held, arrived = refs[:5], refs[5:8], refs[8:12], refs[12]
    copies = []
    for n, target in enumerate(held + (prune,)):
        parts = 4 if n in (1, 3) else 1
        tall = operands[n].shape[0] // parts
        for part in range(parts):
            at = pl.ds(part * tall, tall)
            copy = pltpu.make_async_copy(
                operands[n].at[at], target.at[at], arrived.at[len(copies)]
            )
            copy.start()
            copies.append(copy)
    for copy in copies[:5]:
        copy.wait()
    keep_tiles(held[0], False, held[1], right)
    for copy in copies[5:]:
        copy.wait()
    keep_tiles(held[2], True, held[3], left)


def tiles(*operands):
    held = [pltpu.VMEM(value.shape, value.dtype) for value in operands[:4]]
    return pl.pallas_call(
        tiles_kernel,
        out_shape=[
            jax.ShapeDtypeStruct(operands[n].shape, operands[n].dtype) for n in (1, 3, 4)
        ],
        in_specs=[pl.BlockSpec(memory_space=pltpu.HBM)] * 5,
        out_specs=[VMEM, VMEM, VMEM],
        scratch_shapes=held + [pltpu.SemaphoreType.DMA((11,))],
        compiler_params=room,
        name="tiles",
    )(*(pltpu.with_memory_space_constraint(value, pltpu.HBM) for value in operands))


def call(kernel, name, shapes, *operands, scratch=()):
    return pl.pallas_call(
        kernel,
        out_shape=shapes,
        in_specs=[VMEM] * len(operands),
        out_specs=jax.tree.map(lambda _: VMEM, shapes),
        scratch_shapes=scratch,
        compiler_params=room,
        name=name,
    )(*operands)


def swapped(value, axis, step):
    count = lax.axis_size(axis)
    return lax.ppermute(value, axis, [(i, i ^ step) for i in range(count)])


def pair_kernel(here, beside, out):
    out[0] = here[...]
    out[1] = beside[...]


def stack_kernel(*refs):
    for n, block in enumerate(refs[:-1]):
        refs[-1][n] = block[...]


def hand_kernel(block, after, out):
    out[...] = block[...]


def early_kernel(near, far, rights, after, mask, *refs):
    outs, left, held = refs[:-2], refs[-2], refs[-1]
    layer = lax.axis_index("layer")
    held[0] = near[0]
    held[1 + layer] = near[1]
    held[2 - layer] = far[0]
    held[3] = far[1]
    row, col = lax.axis_index("row"), lax.axis_index("col")
    block = lax.rem(2 * row + 1, 5)
    left[...] = held[row ^ 3 ^ col]
    (rows, depth), broad = left.shape, outs[0].shape[1]
    tall, wide = mask.shape
    share = rows // len(outs)
    lefts = [held[here ^ col] for here in (row, block, block ^ 3)]
    total = jnp.dot(
        jnp.concatenate(lefts, axis=1),
        rights[...].reshape(3 * depth, -1),
        preferred_element_type=jnp.float32,
    )
    for n, out in enumerate(outs):
        out[0:rows, :] = total[:, n * broad : (n + 1) * broad]
        out[rows : out.shape[0] - share, :] = jnp.zeros_like(
            out[rows : out.shape[0] - share, :]
        )
        for i in range(tall):
            kept = entry(mask, i, n % wide).astype(jnp.float32)
            out[rows + i : rows + i + 1, :] = jnp.broadcast_to(kept, (1, broad))
        out[out.shape[0] - share :, :] = left[n * share : (n + 1) * share, :].astype(
            jnp.float32
        )


def last_kernel(inner, outer, out):
    row = lax.axis_index("row")

    @pl.when(jnp.logical_or(row == 1, row == 2))
    def _():
        out[...] = inner[...]

    @pl.when(jnp.logical_or(row == 0, row == 3))
    def _():
        out[...] = outer[...]


def join_kernel(sizes, *refs):
    rows, half, tall, wide = sizes
    count = 2 * wide
    ours, left, theirs = refs[:count], refs[count], refs[count + 1 : -3]
    total, kept, lefts = refs[-3:]
    broad = half // wide
    share = rows // count
    depth = left.shape[1]
    layer = lax.axis_index("layer")
    crossed = jnp.logical_or(lax.axis_index("row") == 1, lax.axis_index("row") == 2)
    here = pl.multiple_of(jnp.where(crossed, depth, 0), depth)
    there = pl.multiple_of(jnp.where(crossed, 0, depth), depth)
    lefts[:, pl.ds(here, depth)] = left[...]
    for n in range(count):
        columns = slice(n * broad, (n + 1) * broad)
        total[:, columns] = ours[n][0:rows, :] + theirs[n][0:rows, :]
        entries = slice(rows, rows + kept.shape[0])
        own = layer == n // wide
        kept[:, columns] = jnp.where(own, ours[n][entries, :], theirs[n][entries, :])
        lefts[n * share : (n + 1) * share, pl.ds(there, depth)] = theirs[n][
            theirs[n].shape[0] - share :, :
        ].astype(left.dtype)


def inflate(side, sizes, joined, out, sums):
    rows, half, tall, wide = sizes
    early, kept, lefts, here, there = joined
    high = rows // tall
    columns = slice(side * half, (side + 1) * half)
    product = early[:, columns] + jnp.dot(
        lefts[...],
        jnp.concatenate([here[:, columns], there[:, columns]], axis=0),
        preferred_element_type=jnp.float32,
    )
    total = jnp.zeros((1, half), jnp.float32)
    for i in range(tall):
        at = slice(i * high, (i + 1) * high)
        keep = jnp.broadcast_to(kept[i : i + 1, columns] != 0.0, (high, half))
        value = jnp.where(keep, product[at, :] * product[at, :], 0.0)
        if out is not None:
            out[at, :] = value
        total += jnp.sum(value, axis=0, keepdims=True)
    sums[...] = total


def sums_kernel(sizes, *refs):
    for core in range(2):

        @pl.when(lax.axis_index("layer") == core)
        def _():
            inflate(1 - core, sizes, refs[:-1], None, refs[-1])


def inflate_kernel(sizes, *refs):
    for core in range(2):

        @pl.when(lax.axis_index("layer") == core)
        def _():
            inflate(core, sizes, refs[:-2], refs[-2], refs[-1])


def on_device(left_blocks, batch_blocks, left_mask, batch_mask, prune_mask):
    f32 = jnp.float32
    rows, columns = left_blocks.shape[0], batch_blocks.shape[2]
    half = columns // 2
    right, left, prune_mask = tiles(
        batch_mask[0],
        batch_blocks[0],
        jnp.transpose(left_mask, (1, 2, 0))[0],
        left_blocks[:, 0, :],
        prune_mask,
    )
    count = lax.axis_size("row")
    first = lax.ppermute(right, "row", [(0, 2), (3, 1), (1, 0), (2, 3)])
    second = lax.ppermute(right, "row", [(0, 1), (3, 2), (1, 3), (2, 0)])
    pairs = [(2, 5), (3, 4), (4, 3), (5, 2), (0, 1), (1, 0), (6, 7), (7, 6)]
    inner = lax.ppermute(right, ("row", "layer"), pairs)
    outer = lax.ppermute(first, "row", [(0, 1), (1, 0), (2, 3), (3, 2)])
    along, across = (
        [(2 * c + core, 2 * (c ^ (2 if core == turn else 1)) + core) for c in range(4) for core in (0, 1)]
        for turn in (1, 0)
    )
    beside = lax.ppermute(left, ("col", "layer"), along)
    pair = call(
        pair_kernel, "pair", jax.ShapeDtypeStruct((2,) + left.shape, left.dtype), left, beside
    )
    piece = jax.ShapeDtypeStruct((rows, half), f32)
    tall, wide = prune_mask.shape
    parts = 2 * wide
    share = rows // parts
    part = jax.ShapeDtypeStruct((rows + (tall + 7) // 8 * 8 + share, columns // parts), f32)
    block = jax.ShapeDtypeStruct(right.shape, right.dtype)
    rights = jax.ShapeDtypeStruct((3,) + right.shape, right.dtype)
    for _ in range(2):
        second = call(hand_kernel, "second", block, second, second)
    rights = call(stack_kernel, "rights", rights, right, first, second)
    handed = call(hand_kernel, "inner", block, inner, rights)
    ours = call(
        early_kernel,
        "early",
        [part] * parts + [jax.ShapeDtypeStruct(left.shape, left.dtype)],
        pair,
        lax.ppermute(pair, ("col", "layer"), across),
        rights,
        handed,
        prune_mask,
        scratch=[pltpu.VMEM((4,) + left.shape, left.dtype)],
    )
    last = call(
        last_kernel, "last", block, handed, outer
    )
    sizes = (rows, half, tall, wide)
    operands = list(call(
        functools.partial(join_kernel, sizes),
        "join",
        [
            jax.ShapeDtypeStruct((rows, columns), f32),
            jax.ShapeDtypeStruct(((tall + 7) // 8 * 8, columns), f32),
            jax.ShapeDtypeStruct((rows, 2 * left.shape[1]), left.dtype),
        ],
        *ours,
        *(swapped(value, "layer", 1) for value in ours[:-1]),
    ))
    operands += [last, swapped(last, "layer", 1)]
    line = jax.ShapeDtypeStruct((1, half), f32)
    sums = call(functools.partial(sums_kernel, sizes), "sums", line, *operands)
    inflated, sums_here = call(
        functools.partial(inflate_kernel, sizes), "inflate", [piece, line], *operands
    )
    total = sums_here
    for step in (1, 2, 3):
        pairs = [
            (2 * z + core, 2 * (z ^ step) + 1 - core)
            for z in range(count)
            for core in range(2)
        ]
        total = total + lax.ppermute(sums, ("row", "layer"), pairs)
    return inflated * (rows * count / (total + epsilon))


def widen(mask, tile_size, dtype):
    first, last = mask.shape
    spread = jnp.broadcast_to(
        mask.astype(dtype)[:, None, :, None], (first, tile_size, last, tile_size)
    )
    return spread.reshape(first * tile_size, last * tile_size)


def on_any_device(left_blocks, batch_blocks, left_mask, batch_mask, prune_mask):
    tile_size = left_blocks.shape[0] // left_mask.shape[0]
    left = left_blocks[:, 0, :] * widen(left_mask[:, 0, :], tile_size, jnp.bfloat16)
    right = batch_blocks[0] * widen(batch_mask[0], tile_size, jnp.bfloat16)
    product = jnp.dot(
        lax.all_gather(left, "col", axis=1, tiled=True),
        lax.all_gather(right, "row", axis=0, tiled=True),
        preferred_element_type=jnp.float32,
    )
    own_share = lax.psum_scatter(product, "layer", scatter_dimension=1, tiled=True)
    inflated = own_share * own_share * widen(prune_mask, tile_size, jnp.float32)
    col_sums = lax.psum(jnp.sum(inflated, axis=0), "row")
    total_rows = left.shape[0] * lax.axis_size("row")
    return inflated * (total_rows / (col_sums + epsilon))


def solution(mesh):
    placed = (
        P("row", "layer", "col"),
        P("layer", "row", "col"),
        P("row", "layer", "col"),
        P("layer", "row", "col"),
        P("row", ("col", "layer")),
    )
    small = mesh.shape["row"] == 4 and mesh.shape["col"] == 4 and mesh.shape["layer"] == 2
    return jax.shard_map(
        on_device if small else on_any_device,
        mesh=mesh,
        in_specs=placed,
        out_specs=P("row", ("col", "layer")),
        check_vma=False,
    )
```
